32 devices in a mesh: kv: 4 (over y, x), blk: 8 (over z, core).
Axes of the slice: x: 2, y: 2, z: 4, core: 2. Of those that a mesh axis runs over, the one named last changes fastest.
Arguments:
- embeds: bfloat16 [3, 64, 4096], P(None, None, 'blk'), may hold values from -6 to 6
- attn_gain: float32 [4096], P('blk'), may hold values from 0.25 to 1.75
- w_query: bfloat16 [4096, 4096], P('blk', 'kv'), may hold values from -0.1875 to 0.1875
- w_key: bfloat16 [4096, 512], P('blk', 'kv'), may hold values from -0.09375 to 0.09375
- w_value: bfloat16 [4096, 512], P('blk', 'kv'), may hold values from -0.09375 to 0.09375
- w_out: bfloat16 [4096, 4096], P('kv', 'blk'), may hold values from -0.375 to 0.375
- cache_kv: bfloat16 [256, 4, 2, 128, 128], P('blk', 'kv'), may hold values from -102 to 102, as said below
- lengths: int32 [64], replicated, may hold values from 1 to 8192, as said below
- block_table: int32 [64, 64], replicated, may hold values from 0 to 256, as said below
- parents: int32 [3, 64], replicated, may hold values from 0 to 63, as said below
Outputs:
- out_rows: bfloat16 [3, 64, 4096], P(None, None, 'blk')
- appended: bfloat16 [3, 64, 4, 2, 128], P(None, 'blk', 'kv')
The draws below stay inside these ranges and needn't reach their ends.
Inputs may be any that keep to these rules, and one draw needn't show every extreme that they name: `lengths`: one beam holds exactly 8192 tokens. `block_table`: row b names the slots of beam b's blocks of 128 tokens in order; entries at and past ceil(lengths[b] / 128) equal 256; no slot is named twice. parents[s, b] lies in the aligned group of 8 beams that holds b. `cache_kv`: slots that no row of block_table names are never read.
All inputs are finite; a program needn't handle non-finite values.
Results may differ from the reference program's by a relative error of at most 0.0044.
The reference program's roundings to bfloat16 on the way count: a program that leaves them out, or rounds other values in their place, can miss the bound.
Values may be sent and summed in bfloat16 or wider, within the bound.
A program may use at most 64 MiB of HBM per device.

```python
import math
import jax
import jax.numpy as jnp
from jax import lax

D = 4096
H = 32
KVH = 4
HD = 128
QPK = 8
GROUP = 8
BLK = 128
MAXLEN = 8192
MAXBLK = 64
STEPS = 3
SPANB = 2
BEAMS = 64
CACHE_SLOT_COUNT = 256


def layout_draw(key):
    base_key = jax.random.fold_in(key, 7177)
    key_count, extended_key, key_tail, key_shuffle = jax.random.split(base_key, 4)
    beam_ids = jnp.arange(BEAMS, dtype=jnp.int32)
    longest = jax.random.randint(extended_key, (), 0, BEAMS)
    counts = jax.random.randint(key_count, (BEAMS,), 1, 2 * SPANB)
    counts = jnp.where(beam_ids == longest, MAXBLK, counts)
    tail_len = jax.random.randint(key_tail, (BEAMS,), 1, BLK + 1)
    token_counts = jnp.where(beam_ids == longest, MAXLEN, (counts - 1) * BLK + tail_len)
    shuffled = jax.random.permutation(key_shuffle, CACHE_SLOT_COUNT).astype(jnp.int32)
    starts = jnp.cumsum(counts) - counts
    block_pos = jnp.arange(MAXBLK, dtype=jnp.int32)
    slot_index = jnp.clip(starts[:, None] + block_pos[None, :], 0, CACHE_SLOT_COUNT - 1)
    slot_table = jnp.where(block_pos[None, :] < counts[:, None], shuffled[slot_index], CACHE_SLOT_COUNT)
    return (token_counts.astype(jnp.int32), slot_table.astype(jnp.int32))


def draw_lengths(key, part):
    return layout_draw(key)[0]


def draw_block_table(key, part):
    return layout_draw(key)[1]


def draw_parents(key, part):
    offsets = jax.random.randint(jax.random.fold_in(key, 3301), (STEPS, BEAMS), 0, GROUP)
    group_base = jnp.arange(BEAMS, dtype=jnp.int32) // GROUP * GROUP
    return (group_base[None, :] + offsets).astype(jnp.int32)


def draw_cache_kv(key, part):
    array_shape = (CACHE_SLOT_COUNT, KVH, 2, BLK, HD)
    key_main = jax.random.fold_in(jax.random.fold_in(key, 5501), 0)
    values = jnp.clip(jax.random.normal(key_main, array_shape, jnp.float32), -6.0, 6.0)
    return values.astype(jnp.bfloat16)


def steps_of(rng, shape, cuts, least, high):
    loudness, own = 1.0, jax.random.fold_in(rng, 6)
    for dim, parts in cuts:
        draws = jnp.exp(jax.random.uniform(jax.random.fold_in(own, dim), (parts,), jnp.float32, least / len(cuts), high / len(cuts)))
        loudness = loudness * jnp.repeat(draws, shape[dim] // parts).reshape([-1 if axis == dim else 1 for axis in range(len(shape))])
    return loudness


def bell_draw(own_key, extent, deviation, limit, cuts=(), kind=jnp.bfloat16):
    result = jax.random.normal(own_key, extent, jnp.float32) * deviation
    if len(cuts) > 0:
        result = steps_of(own_key, extent, cuts, -0.22, 0.18) * result
    return jnp.clip(result, min=-limit, max=limit).astype(kind)


def setup_inputs(seed: int = 0) -> dict:
    splits = jax.random.split(jax.random.key(seed), 11)
    embeds = bell_draw(splits[0], (STEPS, BEAMS, D), 1.0, 6.0, ((2, 8),))
    attn_gain = jnp.clip(1.0 + 0.15 * jax.random.normal(splits[1], (D,), jnp.float32), 0.25, 1.75)
    w_query = bell_draw(splits[2], (D, H * HD), (D // 4) ** -0.5, 0.1875, ((0, 8), (1, 4)))
    w_key = bell_draw(splits[3], (D, KVH * HD), D ** -0.5, 0.09375, ((0, 8), (1, 4)))
    w_value = bell_draw(splits[4], (D, KVH * HD), D ** -0.5, 0.09375, ((0, 8), (1, 4)))
    w_out = bell_draw(splits[5], (H * HD, D), (H * HD // 16) ** -0.5, 0.375, ((0, 4), (1, 8)))
    cache_kv = draw_cache_kv(jax.random.fold_in(splits[10], 71), 0)
    lengths = draw_lengths(jax.random.fold_in(splits[10], 71), 0)
    block_table = draw_block_table(jax.random.fold_in(splits[10], 71), 0)
    parents = draw_parents(jax.random.fold_in(splits[10], 71), 0)
    return {"embeds": embeds, "attn_gain": attn_gain, "w_query": w_query, "w_key": w_key, "w_value": w_value, "w_out": w_out, "cache_kv": cache_kv, "lengths": lengths, "block_table": block_table, "parents": parents}


NEGATIVE = -1e+30
EPSILON = 1e-05
ROPE_BASE = 5000000.0

def rotate(vector, position):
    half_dim = vector.shape[-1] // 2
    exponent = jnp.arange(half_dim, dtype=jnp.float32) * (2.0 / vector.shape[-1])
    frequency = ROPE_BASE ** (-exponent)
    angles = position.astype(jnp.float32)[:, None] * frequency[None, :]
    target_shape = (position.shape[0],) + (1,) * (vector.ndim - 2) + (half_dim,)
    cosines = jnp.cos(angles).reshape(target_shape)
    sine_part = jnp.sin(angles).reshape(target_shape)
    first_half = vector[..., :half_dim]
    second_half = vector[..., half_dim:]
    return jnp.concatenate([first_half * cosines - second_half * sine_part, second_half * cosines + first_half * sine_part], axis=-1)

def attend_beam(beam_id, query_all, recent, root_beams, lengths, block_table, cache_kv):
    scaling = 1.0 / math.sqrt(HD)
    root_beam = root_beams[beam_id]
    length = lengths[root_beam]
    block_count = (length + BLK - 1) // BLK
    beam_query = query_all[beam_id].astype(jnp.float32)
    token_index = jnp.arange(BLK, dtype=jnp.int32)

    def block_scores(block_pos):
        cached = cache_kv[block_table[root_beam, block_pos]].astype(jnp.float32)
        scores = jnp.einsum('gqd,gkd->gqk', beam_query, cached[:, 0]) * scaling
        is_valid = block_pos * BLK + token_index < length
        return (scores, is_valid, cached[:, 1])

    def pass_max(block_pos, running):
        scores, is_valid, unused = block_scores(block_pos)
        return jnp.maximum(running, lax.optimization_barrier(jnp.max(jnp.where(is_valid[None, None, :], scores, NEGATIVE), axis=-1)))
    latest_key_rows = recent[:, beam_id, :, 0].astype(jnp.float32)
    latest_value_rows = recent[:, beam_id, :, 1].astype(jnp.float32)
    recent_scores = jnp.einsum('gqd,tgd->gqt', beam_query, latest_key_rows) * scaling
    ceiling = lax.fori_loop(0, block_count, pass_max, lax.optimization_barrier(jnp.max(recent_scores, axis=-1)))

    def pass_sum(block_pos, running):
        numerator, denominator = running
        scores, is_valid, cached_values = block_scores(block_pos)
        weights = jnp.exp(jnp.where(is_valid[None, None, :], scores - ceiling[..., None], NEGATIVE))
        rounded = lax.optimization_barrier(weights.astype(jnp.bfloat16)).astype(jnp.float32)
        return (numerator + jnp.einsum('gqk,gkd->gqd', rounded, cached_values), denominator + lax.optimization_barrier(jnp.sum(weights, axis=-1)))
    recent_weights = jnp.exp(recent_scores - ceiling[..., None])
    recent_rounded = lax.optimization_barrier(recent_weights.astype(jnp.bfloat16)).astype(jnp.float32)
    start_numer = jnp.einsum('gqt,tgd->gqd', recent_rounded, latest_value_rows)
    start_denom = lax.optimization_barrier(jnp.sum(recent_weights, axis=-1))
    numerator, denominator = lax.fori_loop(0, block_count, pass_sum, (start_numer, start_denom))
    return (numerator / denominator[..., None]).astype(jnp.bfloat16).reshape(H * HD)

def reference(embeds, attn_gain, w_query, w_key, w_value, w_out, cache_kv, lengths, block_table, parents):
    root_beams = jnp.arange(BEAMS, dtype=jnp.int32)
    appended = jnp.zeros((STEPS, BEAMS, KVH, 2, HD), jnp.bfloat16)
    outputs = []
    for step_index in range(STEPS):
        root_beams = root_beams[parents[step_index]]
        appended = appended[:, parents[step_index]]
        stream = embeds[step_index].astype(jnp.float32)
        inverse_rms = lax.rsqrt(lax.optimization_barrier(jnp.mean(stream * stream, axis=1)) + EPSILON)
        normed = (stream * inverse_rms[:, None] * attn_gain[None, :]).astype(jnp.bfloat16)
        position = (lengths[root_beams] + step_index).astype(jnp.int32)
        query_all = rotate(jnp.dot(normed, w_query, preferred_element_type=jnp.float32).reshape(BEAMS, KVH, QPK, HD), position).astype(jnp.bfloat16)
        key_new = rotate(jnp.dot(normed, w_key, preferred_element_type=jnp.float32).reshape(BEAMS, KVH, HD), position).astype(jnp.bfloat16)
        value_new = jnp.dot(normed, w_value, preferred_element_type=jnp.float32).reshape(BEAMS, KVH, HD).astype(jnp.bfloat16)
        appended = appended.at[step_index].set(jnp.stack([key_new, value_new], axis=2))
        recent = appended[:step_index + 1]
        attended = lax.map(lambda beam_id: attend_beam(beam_id, query_all, recent, root_beams, lengths, block_table, cache_kv), jnp.arange(BEAMS, dtype=jnp.int32))
        projected = jnp.dot(attended, w_out, preferred_element_type=jnp.float32)
        outputs.append((stream + projected).astype(jnp.bfloat16))
    return (jnp.stack(outputs), appended)
```

```python
import math

import jax
import jax.numpy as jnp
from jax import lax
from jax.sharding import PartitionSpec as P

GROUP = 8


NEGATIVE = -1e30
EPSILON = 1e-05
ROPE_BASE = 5000000.0


def rotate(vector, position):
    half_dim = vector.shape[-1] // 2
    exponent = jnp.arange(half_dim, dtype=jnp.float32) * (2.0 / vector.shape[-1])
    frequency = ROPE_BASE ** (-exponent)
    angles = position.astype(jnp.float32)[:, None] * frequency[None, :]
    target_shape = (position.shape[0],) + (1,) * (vector.ndim - 2) + (half_dim,)
    cosines = jnp.cos(angles).reshape(target_shape)
    sine_part = jnp.sin(angles).reshape(target_shape)
    first_half = vector[..., :half_dim]
    second_half = vector[..., half_dim:]
    return jnp.concatenate(
        [
            first_half * cosines - second_half * sine_part,
            second_half * cosines + first_half * sine_part,
        ],
        axis=-1,
    )


def pick(table, index):
    count = table.shape[0]
    hit = index[:, None] == jnp.arange(count, dtype=jnp.int32)[None, :]
    return jnp.sum(jnp.where(hit, table[None, :], 0), axis=1)


def body(
    embeds, attn_gain, w_query, w_key, w_value, w_out, cache_kv, lengths, block_table, parents
):
    parts = lax.axis_size("blk")
    shard = lax.axis_index("blk")
    steps, beams, width_part = embeds.shape
    here = beams // parts
    slots = cache_kv.shape[0]
    block_len, hd = cache_kv.shape[3], cache_kv.shape[4]
    heads = w_query.shape[1] // hd
    groups = beams // GROUP
    width = width_part * parts
    scaling = 1.0 / math.sqrt(hd)
    rows = here * steps
    weights = jnp.concatenate([w_query, w_key, w_value], axis=1)
    all_beams = jnp.arange(beams, dtype=jnp.int32)
    roots, origin = [], []
    for s in range(steps):
        before = roots[-1] if s else all_beams
        roots.append(pick(before, parents[s]))
        origin.append([pick(line, parents[s]) for line in (origin[-1] if s else [])] + [all_beams])
    root = jnp.stack(roots, axis=1)
    position = pick(lengths, root.reshape(-1)).reshape(beams, steps) + jnp.arange(
        steps, dtype=jnp.int32
    )
    slot_ids = shard * slots + jnp.arange(slots, dtype=jnp.int32)
    named = block_table[None] == slot_ids[:, None, None]
    code = jnp.arange(block_table.size, dtype=jnp.int32).reshape(block_table.shape) + 1
    code = jnp.sum(jnp.where(named, code[None], 0), axis=(1, 2)) - 1
    filled = code >= 0
    owner = jnp.where(filled, code // block_table.shape[1], -1)
    logical = code % block_table.shape[1]
    slot_length = jnp.where(filled, pick(lengths, jnp.maximum(owner, 0)) - logical * block_len, 0)
    group_of = jnp.maximum(owner, 0) // GROUP

    stream = embeds.astype(jnp.float32)
    squares = lax.psum(jnp.sum(stream * stream, axis=2), "blk")
    inverse = lax.rsqrt(squares / width + EPSILON)
    normed = (stream * inverse[:, :, None] * attn_gain).astype(jnp.bfloat16)
    normed = normed.transpose(1, 0, 2).reshape(beams * steps, width_part)
    projected = lax.psum_scatter(
        jnp.dot(normed, weights, preferred_element_type=jnp.float32),
        "blk",
        scatter_dimension=0,
        tiled=True,
    )
    own_position = lax.dynamic_slice_in_dim(position, shard * here, here).reshape(rows)
    query = rotate(projected[:, : heads * hd].reshape(rows, heads, hd), own_position).astype(
        jnp.bfloat16
    )
    key = rotate(projected[:, heads * hd : (heads + 1) * hd], own_position).astype(jnp.bfloat16)
    value = projected[:, (heads + 1) * hd :].astype(jnp.bfloat16)
    queries = lax.all_gather(query, "blk", axis=0, tiled=True)
    by_group = queries.reshape(groups, GROUP * steps * heads, hd)
    scores = (
        jnp.einsum(
            "sqd,skd->sqk", by_group[group_of], cache_kv[:, 0, 0], preferred_element_type=jnp.float32
        )
        * scaling
    ).reshape(slots, GROUP * steps, heads, block_len)
    root_by_group = root.reshape(groups, GROUP * steps)[group_of]
    active = (
        (root_by_group == owner[:, None])[:, :, None, None]
        & (jnp.arange(block_len, dtype=jnp.int32) < slot_length[:, None])[:, None, None, :]
    )
    slot_top = jnp.max(jnp.where(active, scores, NEGATIVE), axis=-1)
    in_group = (group_of[:, None] == jnp.arange(groups, dtype=jnp.int32)) & filled[:, None]
    group_top = jnp.max(
        jnp.where(in_group[:, :, None, None], slot_top[:, None], NEGATIVE), axis=0
    ).reshape(beams * steps, heads)
    step_of = jnp.arange(rows, dtype=jnp.int32) % steps
    own_origin = jnp.stack(
        [
            jnp.stack([origin[s][u] if u <= s else all_beams * 0 - 1 for u in range(steps)], axis=1)
            for s in range(steps)
        ],
        axis=1,
    )
    own_origin = lax.dynamic_slice_in_dim(own_origin, shard * here, here).reshape(rows, steps)
    beam_of = shard * here + jnp.arange(rows, dtype=jnp.int32) // steps
    linked = jnp.zeros((rows, rows), bool)
    for u in range(steps):
        linked |= (own_origin[:, u : u + 1] == beam_of[None, :]) & (step_of == u)[None, :]
    new_scores = jnp.where(
        linked[:, None, :],
        jnp.einsum("rhd,kd->rhk", query, key, preferred_element_type=jnp.float32) * scaling,
        NEGATIVE,
    )
    own_top = jnp.maximum(
        lax.dynamic_slice_in_dim(group_top, shard * rows, rows), jnp.max(new_scores, axis=-1)
    )
    ceiling = lax.pmax(
        lax.dynamic_update_slice_in_dim(group_top, own_top, shard * rows, 0), "blk"
    )
    slot_ceiling = ceiling.reshape(groups, GROUP * steps, heads)[group_of]
    probs = jnp.exp(jnp.where(active, scores - slot_ceiling[..., None], NEGATIVE))
    slot_denominator = jnp.sum(probs, axis=-1)
    slot_numerator = jnp.einsum(
        "srhk,skd->srhd",
        probs.astype(jnp.bfloat16),
        cache_kv[:, 0, 1],
        preferred_element_type=jnp.float32,
    )
    joined = jnp.concatenate(
        [slot_numerator.reshape(slots, -1), slot_denominator.reshape(slots, -1)], axis=1
    )
    joined = jnp.einsum(
        "sg,sx->gx", in_group.astype(jnp.float32), joined, precision=lax.Precision.HIGHEST
    )
    cut = GROUP * steps * heads * hd
    numerator = lax.psum_scatter(
        joined[:, :cut].reshape(beams * steps, heads, hd), "blk", scatter_dimension=0, tiled=True
    )
    denominator = lax.psum_scatter(
        joined[:, cut:].reshape(beams * steps, heads), "blk", scatter_dimension=0, tiled=True
    )
    own_ceiling = lax.dynamic_slice_in_dim(ceiling, shard * rows, rows)
    new_probs = jnp.exp(new_scores - own_ceiling[..., None])
    numerator += jnp.einsum(
        "rhk,kd->rhd", new_probs.astype(jnp.bfloat16), value, preferred_element_type=jnp.float32
    )
    denominator += jnp.sum(new_probs, axis=-1)
    attended = (numerator / denominator[..., None]).astype(jnp.bfloat16).reshape(rows, heads * hd)
    attended = lax.all_gather(attended, "blk", axis=0, tiled=True)
    partial = jnp.dot(attended, w_out, preferred_element_type=jnp.float32)
    total = lax.psum(partial, "kv").reshape(beams, steps, width_part).transpose(1, 0, 2)
    out = (stream + total).astype(jnp.bfloat16)
    last = own_origin.reshape(here, steps, steps)[:, -1]
    chosen = (
        (last[:, :, None] == beam_of) & (jnp.arange(steps)[None, :, None] == step_of)
    ).astype(jnp.bfloat16)
    appended = jnp.einsum(
        "bur,rcd->ubcd",
        chosen,
        jnp.stack([key, value], axis=1),
        preferred_element_type=jnp.float32,
    ).astype(jnp.bfloat16)
    return out, appended[:, :, None]


def solution(mesh):
    return jax.shard_map(
        body,
        mesh=mesh,
        in_specs=(
            P(None, None, "blk"),
            P("blk"),
            P("blk", "kv"),
            P("blk", "kv"),
            P("blk", "kv"),
            P("kv", "blk"),
            P("blk", "kv", None, None, None),
            P(),
            P(),
            P(),
        ),
        out_specs=(P(None, None, "blk"), P(None, "blk", "kv", None, None)),
        check_vma=False,
    )
```

```python
import functools
import math

import jax
import jax.numpy as jnp
from jax import lax
from jax.experimental import pallas as pl
from jax.experimental.pallas import tpu as pltpu
from jax.sharding import PartitionSpec as P

GROUP = 8


NEGATIVE = -1e30
EPSILON = 1e-05
ROPE_BASE = 5000000.0


MESH = pl.DeviceIdType.MESH


def remote(source, target, send, recv, axis, index):
    return pltpu.make_async_remote_copy(
        src_ref=source,
        dst_ref=target,
        send_sem=send,
        recv_sem=recv,
        device_id={axis: index},
        device_id_type=MESH,
    )


def kernel(
    sizes,
    slot_ref,
    last_ref,
    embeds_ref,
    gain_ref,
    root_ref,
    cos_ref,
    sin_ref,
    linked_ref,
    chosen_ref,
    wq_hbm,
    wk_hbm,
    wv_hbm,
    wo_hbm,
    cache_hbm,
    out_ref,
    appended_ref,
    weights,
    w_out,
    cache,
    stream,
    squares,
    part,
    sib_part,
    z_part,
    q_all,
    scores,
    seg_top,
    tops,
    ceilings,
    seg_num,
    seg_den,
    num,
    den,
    sib_num,
    sib_den,
    z_num,
    z_den,
    att_all,
    out_part,
    kv_part,
    out_rows,
    load_sem,
    sq_send,
    sq_recv,
    sib_send,
    sib_recv,
    z_send,
    z_recv,
    q_send,
    q_recv,
    top_send,
    top_recv,
    nsib_send,
    nsib_recv,
    nz_send,
    nz_recv,
    a_send,
    a_recv,
    kv_send,
    kv_recv,
    o_send,
    o_recv,
):
    n, kvn, steps, here, heads, hd, slots, width = sizes
    me = lax.axis_index("blk")
    kv = lax.axis_index("kv")
    chips = n // 2
    chip, core = me // 2, lax.rem(me, 2)
    sibling = me + 1 - 2 * core
    rows = steps * here
    beams = n * here
    quarter = n * rows // kvn
    lanes = heads * rows
    scaling = 1.0 / math.sqrt(hd)
    wide = w_out.shape[1]

    barrier = pltpu.get_barrier_semaphore()
    for d in range(1, n):
        pl.semaphore_signal(
            barrier, inc=1, device_id={"blk": lax.rem(me + d, n)}, device_id_type=MESH
        )
    for d in range(1, kvn):
        pl.semaphore_signal(
            barrier, inc=1, device_id={"kv": lax.rem(kv + d, kvn)}, device_id_type=MESH
        )
    qw = heads * hd
    loads = [
        pltpu.make_async_copy(wq_hbm, weights.at[:, pl.ds(0, qw)], load_sem.at[0]),
        pltpu.make_async_copy(wk_hbm, weights.at[:, pl.ds(qw, hd)], load_sem.at[1]),
        pltpu.make_async_copy(wv_hbm, weights.at[:, pl.ds(qw + hd, hd)], load_sem.at[2]),
        pltpu.make_async_copy(cache_hbm, cache, load_sem.at[3]),
        pltpu.make_async_copy(wo_hbm, w_out, load_sem.at[4]),
    ]
    for load in loads:
        load.start()

    x = embeds_ref[...].astype(jnp.float32)
    eye = lax.broadcasted_iota(jnp.int32, (beams, beams), 0) == lax.broadcasted_iota(
        jnp.int32, (beams, beams), 1
    )
    for s in range(steps):
        column = jnp.sum(x[s] * x[s], axis=1, keepdims=True)
        squares[0, s : s + 1, 0:beams] = jnp.sum(jnp.where(eye, column, 0.0), axis=0, keepdims=True)
    pl.semaphore_wait(barrier, n - 1 + kvn - 1)
    sends = []
    for d in range(1, n):
        sends.append(
            remote(
                squares.at[0], squares.at[d], sq_send.at[d], sq_recv.at[d], "blk", lax.rem(me + d, n)
            )
        )
        sends[-1].start()
    by_part = x.reshape(steps, n, here, wide).transpose(1, 0, 2, 3).reshape(n * rows, wide)
    stream[...] = by_part
    for send in sends:
        send.wait()
    normed = []
    for s in range(steps):
        total = squares[0, s : s + 1, 0:beams]
        for d in range(1, n):
            total = total + squares[d, s : s + 1, 0:beams]
        column = jnp.sum(jnp.where(eye, total, 0.0), axis=1, keepdims=True)
        normed.append(x[s] * lax.rsqrt(column / width + EPSILON) * gain_ref[...])
    normed = (
        jnp.stack(normed)
        .reshape(steps, chips, 2, here, wide)
        .transpose(2, 1, 0, 3, 4)
        .reshape(2, chips * rows, wide)
        .astype(jnp.bfloat16)
    )
    for load in loads[:3]:
        load.wait()
    for c in range(2):
        part[c] = jnp.dot(
            normed[c], weights[...], preferred_element_type=jnp.float32
        ).reshape(sib_part.shape)
    over = remote(part.at[1 - core], sib_part, sib_send, sib_recv, "blk", sibling)
    over.start()
    over.wait()
    sib_part[...] = part[core] + sib_part[...]
    sends = []
    for d in range(1, chips):
        t = lax.rem(chip + d, chips)
        sends.append(
            remote(
                sib_part.at[t], z_part.at[d], z_send.at[d], z_recv.at[d], "blk", 2 * t + core
            )
        )
        sends[-1].start()
    for send in sends:
        send.wait()
    total = sib_part[chip]
    for d in range(1, chips):
        total = total + z_part[d]

    cos, sin = cos_ref[...], sin_ref[...]

    def rope(block):
        return block * cos + pltpu.roll(block, hd // 2, 1) * sin

    query = jnp.concatenate(
        [rope(total[:, h * hd : (h + 1) * hd]) for h in range(heads)], axis=0
    ).astype(jnp.bfloat16)
    key = rope(total[:, qw : qw + hd]).astype(jnp.bfloat16)
    value = total[:, qw + hd :].astype(jnp.bfloat16)

    def gather(ref, send_sem, recv_sem):
        first = []
        for d in range(1, chips):
            first.append(
                remote(
                    ref.at[me],
                    ref.at[me],
                    send_sem.at[d],
                    recv_sem.at[d],
                    "blk",
                    2 * lax.rem(chip + d, chips) + core,
                )
            )
            first[-1].start()
        second = [remote(ref.at[me], ref.at[me], send_sem.at[0], recv_sem.at[0], "blk", sibling)]
        second[0].start()
        for d in range(1, chips):
            first[d - 1].wait_recv()
            origin = 2 * lax.rem(chip + chips - d, chips) + core
            second.append(
                remote(
                    ref.at[origin],
                    ref.at[origin],
                    send_sem.at[chips + d],
                    recv_sem.at[chips + d],
                    "blk",
                    sibling,
                )
            )
            second[-1].start()
        for copy in second:
            copy.wait()
        for copy in first:
            copy.wait_send()

    q_all[me] = query
    gather(q_all, q_send, q_recv)

    contract_last = (((1,), (1,)), ((), ()))
    contract_first = (((0,), (0,)), ((), ()))
    own_scores = jnp.where(
        linked_ref[...] > 0,
        lax.dot_general(key, query, contract_last, preferred_element_type=jnp.float32) * scaling,
        NEGATIVE,
    )
    own_top = jnp.max(own_scores, axis=0, keepdims=True)
    appended_ref[...] = jnp.dot(
        chosen_ref[...],
        jnp.concatenate([key, value], axis=1),
        preferred_element_type=jnp.float32,
    ).astype(jnp.bfloat16)
    loads[3].wait()
    block = cache.shape[2]
    token = lax.broadcasted_iota(jnp.int32, (block, lanes), 0)

    def look(i, top):
        group = slot_ref[1, i]
        score = (
            lax.dot_general(
                cache[slot_ref[0, i], 0],
                q_all[group],
                contract_last,
                preferred_element_type=jnp.float32,
            )
            * scaling
        )
        active = (root_ref[group] == slot_ref[2, i]) & (token < slot_ref[3, i])
        score = jnp.where(active, score, NEGATIVE)
        scores[i] = score
        kept = jnp.where(slot_ref[4, i] > 0, top, NEGATIVE)
        top = jnp.maximum(kept, jnp.max(score, axis=0, keepdims=True))
        seg_top[i] = top
        return top

    lax.fori_loop(0, slots, look, jnp.full((1, lanes), NEGATIVE, jnp.float32), unroll=4)
    for g in range(n):
        top = jnp.where(last_ref[1, g] > 0, seg_top[last_ref[0, g]], NEGATIVE)
        tops[0, g : g + 1, :] = jnp.where(me == g, jnp.maximum(top, own_top), top)
    sends = []
    for d in range(1, n):
        sends.append(
            remote(tops.at[0], tops.at[d], top_send.at[d], top_recv.at[d], "blk", lax.rem(me + d, n))
        )
        sends[-1].start()
    for send in sends:
        send.wait()
    ceiling = tops[0]
    for d in range(1, n):
        ceiling = jnp.maximum(ceiling, tops[d])
    ceilings[...] = ceiling[:, None, :]

    def add(i, carry):
        total, count = carry
        probs = jnp.exp(scores[i] - ceilings[slot_ref[1, i]])
        same = slot_ref[4, i] > 0
        count = jnp.where(same, count, 0.0) + jnp.sum(probs, axis=0, keepdims=True)
        total = jnp.where(same, total, 0.0) + lax.dot_general(
            probs.astype(jnp.bfloat16),
            cache[slot_ref[0, i], 1],
            contract_first,
            preferred_element_type=jnp.float32,
        )
        seg_num[i] = total
        seg_den[i] = count
        return total, count

    lax.fori_loop(
        0,
        slots,
        add,
        (jnp.zeros((lanes, hd), jnp.float32), jnp.zeros((1, lanes), jnp.float32)),
        unroll=2,
    )
    own_probs = jnp.exp(own_scores - ceilings[me])
    own_num = lax.dot_general(
        own_probs.astype(jnp.bfloat16), value, contract_first, preferred_element_type=jnp.float32
    )
    own_den = jnp.sum(own_probs, axis=0, keepdims=True)
    for t in range(chips):
        for c in range(2):
            g = 2 * t + c
            some = last_ref[1, g] > 0
            num[c, t] = jnp.where(some, seg_num[last_ref[0, g]], 0.0)
            den[c, t] = jnp.where(some, seg_den[last_ref[0, g]], 0.0)
    pair = [
        remote(num.at[1 - core], sib_num, nsib_send.at[0], nsib_recv.at[0], "blk", sibling),
        remote(den.at[1 - core], sib_den, nsib_send.at[1], nsib_recv.at[1], "blk", sibling),
    ]
    for copy in pair:
        copy.start()
    for copy in pair:
        copy.wait()
    sib_num[...] = sib_num[...] + num[core]
    sib_den[...] = sib_den[...] + den[core]
    sends = []
    for d in range(1, chips):
        t = lax.rem(chip + d, chips)
        for k, (source, target) in enumerate(((sib_num, z_num), (sib_den, z_den))):
            sends.append(
                remote(
                    source.at[t],
                    target.at[d],
                    nz_send.at[k, d],
                    nz_recv.at[k, d],
                    "blk",
                    2 * t + core,
                )
            )
            sends[-1].start()
    numerator = own_num + sib_num[chip]
    denominator = own_den + sib_den[chip]
    for send in sends:
        send.wait()
    for d in range(1, chips):
        numerator = numerator + z_num[d]
        denominator = denominator + z_den[d]
    turn = lax.broadcasted_iota(jnp.int32, (lanes, lanes), 0) == lax.broadcasted_iota(
        jnp.int32, (lanes, lanes), 1
    )
    column = jnp.sum(jnp.where(turn, denominator, 0.0), axis=1, keepdims=True)
    att_all[me] = (numerator / column).astype(jnp.bfloat16)
    gather(att_all, a_send, a_recv)

    attended = att_all[...].astype(jnp.float32).reshape(n, heads, rows, hd)
    attended = jnp.concatenate(
        [attended[:, h].reshape(n * rows, hd) for h in range(heads)], axis=1
    ).astype(jnp.bfloat16)
    loads[4].wait()
    out_part[...] = jnp.dot(
        attended, w_out[...], preferred_element_type=jnp.float32
    ).reshape(out_part.shape)
    sends = []
    for d in range(1, kvn):
        t = lax.rem(kv + d, kvn)
        sends.append(
            remote(out_part.at[t], kv_part.at[d], kv_send.at[d], kv_recv.at[d], "kv", t)
        )
        sends[-1].start()
    total = out_part[kv]
    for send in sends:
        send.wait()
    for d in range(1, kvn):
        total = total + kv_part[d]
    start = pl.multiple_of(kv * quarter, 16)
    out_rows[kv] = (stream[pl.ds(start, quarter)] + total).astype(jnp.bfloat16)
    sends = []
    for d in range(1, kvn):
        t = lax.rem(kv + d, kvn)
        sends.append(
            remote(out_rows.at[kv], out_rows.at[kv], o_send.at[d], o_recv.at[d], "kv", t)
        )
        sends[-1].start()
    for send in sends:
        send.wait()
    result = out_rows[...].astype(jnp.float32).reshape(n, steps, here, wide)
    out_ref[...] = result.transpose(1, 0, 2, 3).reshape(steps, beams, wide).astype(jnp.bfloat16)


def pick(table, index):
    count = table.shape[0]
    hit = index[:, None] == jnp.arange(count, dtype=jnp.int32)[None, :]
    return jnp.sum(jnp.where(hit, table[None, :], 0), axis=1)


def body(
    embeds, attn_gain, w_query, w_key, w_value, w_out, cache_kv, lengths, block_table, parents
):
    n = lax.axis_size("blk")
    kvn = lax.axis_size("kv")
    shard = lax.axis_index("blk")
    steps, beams, wide = embeds.shape
    here = beams // n
    slots = cache_kv.shape[0]
    block, hd = cache_kv.shape[3], cache_kv.shape[4]
    heads = w_query.shape[1] // hd
    rows = here * steps
    lanes = heads * rows
    all_beams = jnp.arange(beams, dtype=jnp.int32)
    roots, origin = [], []
    for s in range(steps):
        before = roots[-1] if s else all_beams
        roots.append(pick(before, parents[s]))
        origin.append([pick(line, parents[s]) for line in (origin[-1] if s else [])] + [all_beams])
    root = jnp.stack(roots)
    slot_ids = shard * slots + jnp.arange(slots, dtype=jnp.int32)
    named = block_table[None] == slot_ids[:, None, None]
    code = jnp.arange(block_table.size, dtype=jnp.int32).reshape(block_table.shape) + 1
    code = jnp.sum(jnp.where(named, code[None], 0), axis=(1, 2)) - 1
    filled = code >= 0
    owner = jnp.where(filled, code // block_table.shape[1], -1)
    logical = code % block_table.shape[1]
    tokens = jnp.where(filled, pick(lengths, jnp.maximum(owner, 0)) - logical * block, 0)
    group = jnp.where(filled, owner // GROUP, n - 1)
    place = jnp.arange(slots, dtype=jnp.int32)
    rank = jnp.sum(
        (group[None, :] < group[:, None])
        | ((group[None, :] == group[:, None]) & (place[None, :] < place[:, None])),
        axis=1,
    )
    table = jnp.stack([place, group, owner, tokens])
    table = jnp.sum(jnp.where((rank[:, None] == place[None, :])[None], table[:, :, None], 0), axis=1)
    same = jnp.concatenate(
        [jnp.zeros((1,), jnp.int32), (table[1, 1:] == table[1, :-1]).astype(jnp.int32)]
    )
    table = jnp.concatenate([table, same[None]])
    upto = jnp.sum(group[None, :] <= jnp.arange(n, dtype=jnp.int32)[:, None], axis=1)
    held = jnp.sum(group[None, :] == jnp.arange(n, dtype=jnp.int32)[:, None], axis=1)
    last = jnp.stack([jnp.maximum(upto - 1, 0), held]).astype(jnp.int32)

    root_rows = root.reshape(steps, n, here).transpose(1, 0, 2).reshape(n, 1, 1, rows)
    root_rows = jnp.broadcast_to(root_rows, (n, 1, heads, rows)).reshape(n, 1, lanes)
    own = lax.dynamic_slice_in_dim(root, shard * here, here, 1)
    position = pick(lengths, own.reshape(-1)).reshape(steps, here) + jnp.arange(
        steps, dtype=jnp.int32
    )[:, None]
    exponent = jnp.arange(hd // 2, dtype=jnp.float32) * (2.0 / hd)
    angles = position.reshape(rows).astype(jnp.float32)[:, None] * (ROPE_BASE ** (-exponent))
    cos, sin = jnp.cos(angles), jnp.sin(angles)
    cos = jnp.concatenate([cos, cos], axis=1)
    sin = jnp.concatenate([-sin, sin], axis=1)
    origin_own = jnp.stack(
        [
            jnp.stack([origin[s][u] if u <= s else all_beams * 0 - 1 for u in range(steps)])
            for s in range(steps)
        ]
    )
    origin_own = lax.dynamic_slice_in_dim(origin_own, shard * here, here, 2) - shard * here
    seat = jnp.arange(here, dtype=jnp.int32)
    meets = origin_own.transpose(0, 2, 1)[:, :, :, None] == seat
    linked = meets.transpose(2, 3, 0, 1).reshape(rows, 1, rows)
    linked = jnp.broadcast_to(linked, (rows, heads, rows)).reshape(rows, lanes).astype(jnp.float32)
    chosen = meets[-1].transpose(1, 0, 2)[:, :, None, :] & (
        jnp.arange(steps)[:, None, None, None] == jnp.arange(steps)[None, None, :, None]
    )
    chosen = chosen.reshape(rows, rows).astype(jnp.bfloat16)

    chips = n // 2
    total_rows = n * rows
    columns = (heads + 2) * hd
    quarter = total_rows // kvn
    sizes = (n, kvn, steps, here, heads, hd, slots, wide * n)
    bf16, f32 = jnp.bfloat16, jnp.float32
    dma = pltpu.SemaphoreType.DMA
    lane_room = -(-beams // 128) * 128
    vmem = pl.BlockSpec(memory_space=pltpu.VMEM)
    smem = pl.BlockSpec(memory_space=pltpu.SMEM)
    hbm = pl.BlockSpec(memory_space=pl.ANY)
    out, appended = pl.pallas_call(
        functools.partial(kernel, sizes),
        out_shape=(
            jax.ShapeDtypeStruct((steps, beams, wide), bf16),
            jax.ShapeDtypeStruct((rows, 2 * hd), bf16),
        ),
        in_specs=[smem, smem] + [vmem] * 7 + [hbm] * 5,
        out_specs=(vmem, vmem),
        scratch_shapes=[
            pltpu.VMEM((wide, columns), bf16),
            pltpu.VMEM((heads * hd, wide), bf16),
            pltpu.VMEM((slots, 2, block, hd), bf16),
            pltpu.VMEM((total_rows, wide), f32),
            pltpu.VMEM((n, 8, lane_room), f32),
            pltpu.VMEM((2, chips, rows, columns), f32),
            pltpu.VMEM((chips, rows, columns), f32),
            pltpu.VMEM((chips, rows, columns), f32),
            pltpu.VMEM((n, lanes, hd), bf16),
            pltpu.VMEM((slots, block, lanes), f32),
            pltpu.VMEM((slots, 1, lanes), f32),
            pltpu.VMEM((n, n, lanes), f32),
            pltpu.VMEM((n, 1, lanes), f32),
            pltpu.VMEM((slots, lanes, hd), f32),
            pltpu.VMEM((slots, 1, lanes), f32),
            pltpu.VMEM((2, chips, lanes, hd), f32),
            pltpu.VMEM((2, chips, 1, lanes), f32),
            pltpu.VMEM((chips, lanes, hd), f32),
            pltpu.VMEM((chips, 1, lanes), f32),
            pltpu.VMEM((chips, lanes, hd), f32),
            pltpu.VMEM((chips, 1, lanes), f32),
            pltpu.VMEM((n, lanes, hd), bf16),
            pltpu.VMEM((kvn, quarter, wide), f32),
            pltpu.VMEM((kvn, quarter, wide), f32),
            pltpu.VMEM((kvn, quarter, wide), bf16),
            dma((5,)),
            dma((n,)),
            dma((n,)),
            dma,
            dma,
            dma((chips,)),
            dma((chips,)),
            dma((n,)),
            dma((n,)),
            dma((n,)),
            dma((n,)),
            dma((2,)),
            dma((2,)),
            dma((2, chips)),
            dma((2, chips)),
            dma((n,)),
            dma((n,)),
            dma((kvn,)),
            dma((kvn,)),
            dma((kvn,)),
            dma((kvn,)),
        ],
        compiler_params=pltpu.CompilerParams(
            collective_id=0, has_side_effects=True, vmem_limit_bytes=60 * 1024 * 1024
        ),
    )(
        table,
        last,
        embeds,
        attn_gain[None, :],
        root_rows,
        cos,
        sin,
        linked,
        chosen,
        w_query,
        w_key,
        w_value,
        w_out,
        cache_kv.reshape(slots, 2, block, hd),
    )
    return out, appended.reshape(steps, here, 1, 2, hd)


def solution(mesh):
    return jax.shard_map(
        body,
        mesh=mesh,
        in_specs=(
            P(None, None, "blk"),
            P("blk"),
            P("blk", "kv"),
            P("blk", "kv"),
            P("blk", "kv"),
            P("kv", "blk"),
            P("blk", "kv", None, None, None),
            P(),
            P(),
            P(),
        ),
        out_specs=(P(None, None, "blk"), P(None, "blk", "kv", None, None)),
        check_vma=False,
    )
```

```python
import functools
import math

import jax
import jax.numpy as jnp
from jax import lax
from jax.experimental import pallas as pl
from jax.experimental.pallas import tpu as pltpu
from jax.sharding import PartitionSpec as P

GROUP = 8


NEGATIVE = -1e30
EPSILON = 1e-05
ROPE_BASE = 5000000.0


MESH = pl.DeviceIdType.MESH


def remote(source, target, send, recv, axis, index):
    return pltpu.make_async_remote_copy(
        src_ref=source,
        dst_ref=target,
        send_sem=send,
        recv_sem=recv,
        device_id={axis: index},
        device_id_type=MESH,
    )


def kernel(
    sizes,
    slot_ref,
    last_ref,
    embeds_ref,
    gain_ref,
    root_ref,
    cos_ref,
    sin_ref,
    linked_ref,
    chosen_ref,
    wq_hbm,
    wk_hbm,
    wv_hbm,
    wo_hbm,
    cache_hbm,
    out_ref,
    appended_ref,
    weights,
    w_out,
    cache,
    stream,
    squares,
    part_a,
    part_b,
    sib_a,
    sib_b,
    z_a,
    z_b,
    turned,
    q_a,
    q_b,
    scores,
    seg_top,
    tops,
    ceilings,
    seg_num,
    seg_den,
    num,
    den,
    sib_num,
    sib_den,
    low_num,
    z_num,
    z_den,
    att_all,
    out_part,
    kv_part,
    out_rows,
    load_sem,
    sq_send,
    sq_recv,
    sib_send,
    sib_recv,
    z_send,
    z_recv,
    q_send,
    q_recv,
    top_send,
    top_recv,
    nsib_send,
    nsib_recv,
    nz_send,
    nz_recv,
    a_send,
    a_recv,
    kv_send,
    kv_recv,
    o_send,
    o_recv,
):
    n, kvn, steps, here, heads, hd, slots, width = sizes
    me = lax.axis_index("blk")
    kv = lax.axis_index("kv")
    chips = n // 2
    chip, core = me // 2, lax.rem(me, 2)
    sibling = me + 1 - 2 * core
    rows = steps * here
    beams = n * here
    quarter = n * rows // kvn
    half = heads // 2
    lanes = half * rows
    q_all = (q_a, q_b)
    parts, sib_parts, z_parts = (part_a, part_b), (sib_a, sib_b), (z_a, z_b)
    scaling = 1.0 / math.sqrt(hd)
    wide = w_out.shape[1]

    barrier = pltpu.get_barrier_semaphore()
    for d in range(1, n):
        pl.semaphore_signal(
            barrier, inc=1, device_id={"blk": lax.rem(me + d, n)}, device_id_type=MESH
        )
    for d in range(1, kvn):
        pl.semaphore_signal(
            barrier, inc=1, device_id={"kv": lax.rem(kv + d, kvn)}, device_id_type=MESH
        )
    hw = half * hd
    loads = [
        pltpu.make_async_copy(
            wq_hbm.at[:, pl.ds(0, hw)], weights.at[:, pl.ds(0, hw)], load_sem.at[0]
        ),
        pltpu.make_async_copy(wk_hbm, weights.at[:, pl.ds(hw, hd)], load_sem.at[1]),
        pltpu.make_async_copy(wv_hbm, weights.at[:, pl.ds(hw + hd, hd)], load_sem.at[2]),
        pltpu.make_async_copy(
            wq_hbm.at[:, pl.ds(hw, hw)], weights.at[:, pl.ds(hw + 2 * hd, hw)], load_sem.at[3]
        ),
        pltpu.make_async_copy(cache_hbm, cache, load_sem.at[4]),
        pltpu.make_async_copy(wo_hbm, w_out, load_sem.at[5]),
    ]
    for load in loads:
        load.start()

    x = embeds_ref[...].astype(jnp.float32)
    eye = lax.broadcasted_iota(jnp.int32, (beams, beams), 0) == lax.broadcasted_iota(
        jnp.int32, (beams, beams), 1
    )
    for s in range(steps):
        column = jnp.sum(x[s] * x[s], axis=1, keepdims=True)
        squares[0, s : s + 1, 0:beams] = jnp.sum(jnp.where(eye, column, 0.0), axis=0, keepdims=True)
    pl.semaphore_wait(barrier, n - 1 + kvn - 1)
    sends = []
    for d in range(1, n):
        sends.append(
            remote(
                squares.at[0], squares.at[d], sq_send.at[d], sq_recv.at[d], "blk", lax.rem(me + d, n)
            )
        )
        sends[-1].start()
    by_part = x.reshape(steps, n, here, wide).transpose(1, 0, 2, 3).reshape(n * rows, wide)
    stream[...] = by_part
    for send in sends:
        send.wait()
    normed = []
    for s in range(steps):
        total = squares[0, s : s + 1, 0:beams]
        for d in range(1, n):
            total = total + squares[d, s : s + 1, 0:beams]
        column = jnp.sum(jnp.where(eye, total, 0.0), axis=1, keepdims=True)
        normed.append(x[s] * lax.rsqrt(column / width + EPSILON) * gain_ref[...])
    normed = (
        jnp.stack(normed)
        .reshape(steps, chips, 2, here, wide)
        .transpose(2, 1, 0, 3, 4)
        .reshape(2, chips * rows, wide)
        .astype(jnp.bfloat16)
    )
    for load in loads[:4]:
        load.wait()

    def across(source, target, send_sem, recv_sem):
        copies = []
        for d in range(1, chips):
            t = lax.rem(chip + d, chips)
            copies.append(
                remote(
                    source.at[t], target.at[d], send_sem.at[d], recv_sem.at[d], "blk", 2 * t + core
                )
            )
            copies[-1].start()
        return copies

    over = []
    first_column = 0
    for k in range(2):
        span = parts[k].shape[-1]
        for c in range(2):
            parts[k][c] = jnp.dot(
                normed[c],
                weights[:, first_column : first_column + span],
                preferred_element_type=jnp.float32,
            ).reshape(sib_parts[k].shape)
        first_column += span
        over.append(
            remote(
                parts[k].at[1 - core], sib_parts[k], sib_send.at[k], sib_recv.at[k], "blk", sibling
            )
        )
        over[k].start()
    crossing = []
    for k in range(2):
        over[k].wait()
        sib_parts[k][...] = parts[k][core] + sib_parts[k][...]
        crossing.append(across(sib_parts[k], z_parts[k], z_send.at[k], z_recv.at[k]))
    loads[4].wait()

    def turn_values(i, carry):
        turned[i] = cache[i, 1].astype(jnp.float32).T.astype(jnp.bfloat16)
        return carry

    lax.fori_loop(0, slots, turn_values, 0, unroll=2)
    cos, sin = cos_ref[...], sin_ref[...]

    def rope(block):
        return block * cos + pltpu.roll(block, hd // 2, 1) * sin

    def arrived(k):
        for copy in crossing[k]:
            copy.wait()
        total = sib_parts[k][chip]
        for d in range(1, chips):
            total = total + z_parts[k][d]
        return total

    def spread(ref, send_sem, recv_sem):
        direct = []
        for d in range(1, chips):
            peer = 2 * lax.rem(chip + d, chips) + core
            direct.append(
                remote(ref.at[me], ref.at[me], send_sem.at[d], recv_sem.at[d], "blk", peer)
            )
            direct[-1].start()
        to_sibling = remote(
            ref.at[me], ref.at[me], send_sem.at[0], recv_sem.at[0], "blk", sibling
        )
        to_sibling.start()
        return direct, [to_sibling]

    def relay(ref, send_sem, recv_sem, copies):
        for d in range(1, chips):
            copies[0][d - 1].wait_recv()
            origin = 2 * lax.rem(chip + chips - d, chips) + core
            copies[1].append(
                remote(
                    ref.at[origin],
                    ref.at[origin],
                    send_sem.at[chips + d],
                    recv_sem.at[chips + d],
                    "blk",
                    sibling,
                )
            )
            copies[1][-1].start()

    def finish(copies):
        for copy in copies[1]:
            copy.wait()
        for copy in copies[0]:
            copy.wait_send()

    def turn_query(total):
        return jnp.concatenate(
            [rope(total[:, h * hd : (h + 1) * hd]) for h in range(half)], axis=0
        ).astype(jnp.bfloat16)

    queries, gathers = [None, None], [None, None]
    total = arrived(0)
    queries[0] = turn_query(total)
    q_all[0][me] = queries[0]
    gathers[0] = spread(q_all[0], q_send.at[0], q_recv.at[0])
    key = rope(total[:, half * hd : (half + 1) * hd]).astype(jnp.bfloat16)
    value_wide = total[:, (half + 1) * hd :]
    value = value_wide.astype(jnp.bfloat16)
    value_turned = value_wide.T.astype(jnp.bfloat16)
    appended_ref[...] = jnp.dot(
        chosen_ref[...],
        jnp.concatenate([key, value], axis=1),
        preferred_element_type=jnp.float32,
    ).astype(jnp.bfloat16)
    queries[1] = turn_query(arrived(1))
    q_all[1][me] = queries[1]
    gathers[1] = spread(q_all[1], q_send.at[1], q_recv.at[1])
    relay(q_all[0], q_send.at[0], q_recv.at[0], gathers[0])

    contract_last = (((1,), (1,)), ((), ()))
    block = cache.shape[2]
    token = lax.broadcasted_iota(jnp.int32, (block, lanes), 0)
    own_scores, top_sends = [], []
    for k in range(2):
        own_scores.append(
            jnp.where(
                linked_ref[...] > 0,
                lax.dot_general(
                    key, queries[k], contract_last, preferred_element_type=jnp.float32
                )
                * scaling,
                NEGATIVE,
            )
        )
        own_top = jnp.max(own_scores[k], axis=0, keepdims=True)
        finish(gathers[k])

        def look(i, top):
            group = slot_ref[1, i]
            score = (
                lax.dot_general(
                    cache[slot_ref[0, i], 0],
                    q_all[k][group],
                    contract_last,
                    preferred_element_type=jnp.float32,
                )
                * scaling
            )
            limit = jnp.where(root_ref[group] == slot_ref[2, i], slot_ref[3, i], 0)
            score = jnp.where(token < limit, score, NEGATIVE)
            scores[k, i] = score
            kept = jnp.where(slot_ref[4, i] > 0, top, NEGATIVE)
            top = jnp.maximum(kept, jnp.max(score, axis=0, keepdims=True))
            seg_top[i] = top
            return top

        lax.fori_loop(0, slots, look, jnp.full((1, lanes), NEGATIVE, jnp.float32), unroll=8)
        for g in range(n):
            top = jnp.where(last_ref[1, g] > 0, seg_top[last_ref[0, g]], NEGATIVE)
            tops[k, 0, g : g + 1, :] = jnp.where(me == g, jnp.maximum(top, own_top), top)
        copies = []
        for d in range(1, n):
            copies.append(
                remote(
                    tops.at[k, 0],
                    tops.at[k, d],
                    top_send.at[k, d],
                    top_recv.at[k, d],
                    "blk",
                    lax.rem(me + d, n),
                )
            )
            copies[-1].start()
        top_sends.append(copies)
        if k == 0:
            relay(q_all[1], q_send.at[1], q_recv.at[1], gathers[1])

    pairs, own_nums, own_dens = [], [], []

    def attend(k):
        for copy in top_sends[k]:
            copy.wait()
        ceiling = tops[k, 0]
        for d in range(1, n):
            ceiling = jnp.maximum(ceiling, tops[k, d])
        ceilings[...] = ceiling[:, None, :]

        def add(i, carry):
            total, count = carry
            probs = jnp.exp(scores[k, i] - ceilings[slot_ref[1, i]])
            same = slot_ref[4, i] > 0
            count = jnp.where(same, count, 0.0) + jnp.sum(probs, axis=0, keepdims=True)
            total = jnp.where(same, total, 0.0) + jnp.dot(
                turned[slot_ref[0, i]],
                probs.astype(jnp.bfloat16),
                preferred_element_type=jnp.float32,
            )
            seg_num[i] = total
            seg_den[i] = count
            return total, count

        lax.fori_loop(
            0,
            slots,
            add,
            (jnp.zeros((hd, lanes), jnp.float32), jnp.zeros((1, lanes), jnp.float32)),
            unroll=4,
        )
        own_probs = jnp.exp(own_scores[k] - ceilings[me])
        own_nums.append(
            jnp.dot(
                value_turned, own_probs.astype(jnp.bfloat16), preferred_element_type=jnp.float32
            ).T
        )
        own_dens.append(jnp.sum(own_probs, axis=0, keepdims=True))
        for t in range(chips):
            for c in range(2):
                g = 2 * t + c
                some = last_ref[1, g] > 0
                num[k, c, t] = jnp.where(some, seg_num[last_ref[0, g]], 0.0).T
                den[k, c, t] = jnp.where(some, seg_den[last_ref[0, g]], 0.0)
        pair = [
            remote(
                num.at[k, 1 - core],
                sib_num.at[k],
                nsib_send.at[k, 0],
                nsib_recv.at[k, 0],
                "blk",
                sibling,
            ),
            remote(
                den.at[k, 1 - core],
                sib_den.at[k],
                nsib_send.at[k, 1],
                nsib_recv.at[k, 1],
                "blk",
                sibling,
            ),
        ]
        for copy in pair:
            copy.start()
        pairs.append(pair)

    def send_sums(k):
        for copy in pairs[k]:
            copy.wait()
        sib_num[k] = sib_num[k] + num[k, core]
        sib_den[k] = sib_den[k] + den[k, core]
        low_num[k] = sib_num[k].astype(jnp.bfloat16)
        return across(low_num.at[k], z_num.at[k], nz_send.at[k, 0], nz_recv.at[k, 0]) + across(
            sib_den.at[k], z_den.at[k], nz_send.at[k, 1], nz_recv.at[k, 1]
        )

    turn = lax.broadcasted_iota(jnp.int32, (lanes, lanes), 0) == lax.broadcasted_iota(
        jnp.int32, (lanes, lanes), 1
    )

    def close(k, copies):
        for copy in copies:
            copy.wait()
        numerator = own_nums[k] + sib_num[k, chip]
        denominator = own_dens[k] + sib_den[k, chip]
        for d in range(1, chips):
            numerator = numerator + z_num[k, d].astype(jnp.float32)
            denominator = denominator + z_den[k, d]
        column = jnp.sum(jnp.where(turn, denominator, 0.0), axis=1, keepdims=True)
        att_all[k, me] = (numerator / column).astype(jnp.bfloat16)
        return spread(att_all.at[k], a_send.at[k], a_recv.at[k])

    attend(0)
    sums = [send_sums(0)]
    attend(1)
    gathers = [close(0, sums[0])]
    sums.append(send_sums(1))
    relay(att_all.at[0], a_send.at[0], a_recv.at[0], gathers[0])
    gathers.append(close(1, sums[1]))
    loads[5].wait()

    def project(k):
        finish(gathers[k])
        attended = att_all[k].astype(jnp.float32).reshape(n, half, rows, hd)
        attended = jnp.concatenate(
            [attended[:, h].reshape(n * rows, hd) for h in range(half)], axis=1
        ).astype(jnp.bfloat16)
        return jnp.dot(
            attended,
            w_out[k * half * hd : (k + 1) * half * hd, :],
            preferred_element_type=jnp.float32,
        )

    early = project(0)
    relay(att_all.at[1], a_send.at[1], a_recv.at[1], gathers[1])
    out_part[...] = (early + project(1)).reshape(out_part.shape)
    sends = []
    for d in range(1, kvn):
        t = lax.rem(kv + d, kvn)
        sends.append(
            remote(out_part.at[t], kv_part.at[d], kv_send.at[d], kv_recv.at[d], "kv", t)
        )
        sends[-1].start()
    total = out_part[kv]
    for send in sends:
        send.wait()
    for d in range(1, kvn):
        total = total + kv_part[d]
    start = pl.multiple_of(kv * quarter, 16)
    out_rows[kv] = (stream[pl.ds(start, quarter)] + total).astype(jnp.bfloat16)
    sends = []
    for d in range(1, kvn):
        t = lax.rem(kv + d, kvn)
        sends.append(
            remote(out_rows.at[kv], out_rows.at[kv], o_send.at[d], o_recv.at[d], "kv", t)
        )
        sends[-1].start()
    for send in sends:
        send.wait()
    result = out_rows[...].astype(jnp.float32).reshape(n, steps, here, wide)
    out_ref[...] = result.transpose(1, 0, 2, 3).reshape(steps, beams, wide).astype(jnp.bfloat16)


def pick(table, index):
    count = table.shape[0]
    hit = index[:, None] == jnp.arange(count, dtype=jnp.int32)[None, :]
    return jnp.sum(jnp.where(hit, table[None, :], 0), axis=1)


def body(
    embeds, attn_gain, w_query, w_key, w_value, w_out, cache_kv, lengths, block_table, parents
):
    n = lax.axis_size("blk")
    kvn = lax.axis_size("kv")
    shard = lax.axis_index("blk")
    steps, beams, wide = embeds.shape
    here = beams // n
    slots = cache_kv.shape[0]
    block, hd = cache_kv.shape[3], cache_kv.shape[4]
    heads = w_query.shape[1] // hd
    rows = here * steps
    half = heads // 2
    lanes = half * rows
    all_beams = jnp.arange(beams, dtype=jnp.int32)
    roots, origin = [], []
    for s in range(steps):
        before = roots[-1] if s else all_beams
        roots.append(pick(before, parents[s]))
        origin.append([pick(line, parents[s]) for line in (origin[-1] if s else [])] + [all_beams])
    root = jnp.stack(roots)
    slot_ids = shard * slots + jnp.arange(slots, dtype=jnp.int32)
    named = block_table[None] == slot_ids[:, None, None]
    code = jnp.arange(block_table.size, dtype=jnp.int32).reshape(block_table.shape) + 1
    code = jnp.sum(jnp.where(named, code[None], 0), axis=(1, 2)) - 1
    filled = code >= 0
    owner = jnp.where(filled, code // block_table.shape[1], -1)
    logical = code % block_table.shape[1]
    tokens = jnp.where(filled, pick(lengths, jnp.maximum(owner, 0)) - logical * block, 0)
    group = jnp.where(filled, owner // GROUP, n - 1)
    place = jnp.arange(slots, dtype=jnp.int32)
    rank = jnp.sum(
        (group[None, :] < group[:, None])
        | ((group[None, :] == group[:, None]) & (place[None, :] < place[:, None])),
        axis=1,
    )
    table = jnp.stack([place, group, owner, tokens])
    table = jnp.sum(jnp.where((rank[:, None] == place[None, :])[None], table[:, :, None], 0), axis=1)
    same = jnp.concatenate(
        [jnp.zeros((1,), jnp.int32), (table[1, 1:] == table[1, :-1]).astype(jnp.int32)]
    )
    table = jnp.concatenate([table, same[None]])
    upto = jnp.sum(group[None, :] <= jnp.arange(n, dtype=jnp.int32)[:, None], axis=1)
    held = jnp.sum(group[None, :] == jnp.arange(n, dtype=jnp.int32)[:, None], axis=1)
    last = jnp.stack([jnp.maximum(upto - 1, 0), held]).astype(jnp.int32)

    root_rows = root.reshape(steps, n, here).transpose(1, 0, 2).reshape(n, 1, 1, rows)
    root_rows = jnp.broadcast_to(root_rows, (n, 1, half, rows)).reshape(n, 1, lanes)
    own = lax.dynamic_slice_in_dim(root, shard * here, here, 1)
    position = pick(lengths, own.reshape(-1)).reshape(steps, here) + jnp.arange(
        steps, dtype=jnp.int32
    )[:, None]
    exponent = jnp.arange(hd // 2, dtype=jnp.float32) * (2.0 / hd)
    angles = position.reshape(rows).astype(jnp.float32)[:, None] * (ROPE_BASE ** (-exponent))
    cos, sin = jnp.cos(angles), jnp.sin(angles)
    cos = jnp.concatenate([cos, cos], axis=1)
    sin = jnp.concatenate([-sin, sin], axis=1)
    origin_own = jnp.stack(
        [
            jnp.stack([origin[s][u] if u <= s else all_beams * 0 - 1 for u in range(steps)])
            for s in range(steps)
        ]
    )
    origin_own = lax.dynamic_slice_in_dim(origin_own, shard * here, here, 2) - shard * here
    seat = jnp.arange(here, dtype=jnp.int32)
    meets = origin_own.transpose(0, 2, 1)[:, :, :, None] == seat
    linked = meets.transpose(2, 3, 0, 1).reshape(rows, 1, rows)
    linked = jnp.broadcast_to(linked, (rows, half, rows)).reshape(rows, lanes).astype(jnp.float32)
    chosen = meets[-1].transpose(1, 0, 2)[:, :, None, :] & (
        jnp.arange(steps)[:, None, None, None] == jnp.arange(steps)[None, None, :, None]
    )
    chosen = chosen.reshape(rows, rows).astype(jnp.bfloat16)

    chips = n // 2
    total_rows = n * rows
    columns = (heads + 2) * hd
    quarter = total_rows // kvn
    sizes = (n, kvn, steps, here, heads, hd, slots, wide * n)
    bf16, f32 = jnp.bfloat16, jnp.float32
    dma = pltpu.SemaphoreType.DMA
    lane_room = -(-beams // 128) * 128
    vmem = pl.BlockSpec(memory_space=pltpu.VMEM)
    smem = pl.BlockSpec(memory_space=pltpu.SMEM)
    hbm = pl.BlockSpec(memory_space=pl.ANY)
    out, appended = pl.pallas_call(
        functools.partial(kernel, sizes),
        out_shape=(
            jax.ShapeDtypeStruct((steps, beams, wide), bf16),
            jax.ShapeDtypeStruct((rows, 2 * hd), bf16),
        ),
        in_specs=[smem, smem] + [vmem] * 7 + [hbm] * 5,
        out_specs=(vmem, vmem),
        scratch_shapes=[
            pltpu.VMEM((wide, columns), bf16),
            pltpu.VMEM((heads * hd, wide), bf16),
            pltpu.VMEM((slots, 2, block, hd), bf16),
            pltpu.VMEM((total_rows, wide), f32),
            pltpu.VMEM((n, 8, lane_room), f32),
            pltpu.VMEM((2, chips, rows, (half + 2) * hd), f32),
            pltpu.VMEM((2, chips, rows, half * hd), f32),
            pltpu.VMEM((chips, rows, (half + 2) * hd), f32),
            pltpu.VMEM((chips, rows, half * hd), f32),
            pltpu.VMEM((chips, rows, (half + 2) * hd), f32),
            pltpu.VMEM((chips, rows, half * hd), f32),
            pltpu.VMEM((slots, hd, block), bf16),
            pltpu.VMEM((n, lanes, hd), bf16),
            pltpu.VMEM((n, lanes, hd), bf16),
            pltpu.VMEM((2, slots, block, lanes), f32),
            pltpu.VMEM((slots, 1, lanes), f32),
            pltpu.VMEM((2, n, n, lanes), f32),
            pltpu.VMEM((n, 1, lanes), f32),
            pltpu.VMEM((slots, hd, lanes), f32),
            pltpu.VMEM((slots, 1, lanes), f32),
            pltpu.VMEM((2, 2, chips, lanes, hd), f32),
            pltpu.VMEM((2, 2, chips, 1, lanes), f32),
            pltpu.VMEM((2, chips, lanes, hd), f32),
            pltpu.VMEM((2, chips, 1, lanes), f32),
            pltpu.VMEM((2, chips, lanes, hd), bf16),
            pltpu.VMEM((2, chips, lanes, hd), bf16),
            pltpu.VMEM((2, chips, 1, lanes), f32),
            pltpu.VMEM((2, n, lanes, hd), bf16),
            pltpu.VMEM((kvn, quarter, wide), f32),
            pltpu.VMEM((kvn, quarter, wide), f32),
            pltpu.VMEM((kvn, quarter, wide), bf16),
            dma((6,)),
            dma((n,)),
            dma((n,)),
            dma((2,)),
            dma((2,)),
            dma((2, chips)),
            dma((2, chips)),
            dma((2, n)),
            dma((2, n)),
            dma((2, n)),
            dma((2, n)),
            dma((2, 2)),
            dma((2, 2)),
            dma((2, 2, chips)),
            dma((2, 2, chips)),
            dma((2, n)),
            dma((2, n)),
            dma((kvn,)),
            dma((kvn,)),
            dma((kvn,)),
            dma((kvn,)),
        ],
        compiler_params=pltpu.CompilerParams(
            collective_id=0, has_side_effects=True, vmem_limit_bytes=60 * 1024 * 1024
        ),
    )(
        table,
        last,
        embeds,
        attn_gain[None, :],
        root_rows,
        cos,
        sin,
        linked,
        chosen,
        w_query,
        w_key,
        w_value,
        w_out,
        cache_kv.reshape(slots, 2, block, hd),
    )
    return out, appended.reshape(steps, here, 1, 2, hd)


def solution(mesh):
    return jax.shard_map(
        body,
        mesh=mesh,
        in_specs=(
            P(None, None, "blk"),
            P("blk"),
            P("blk", "kv"),
            P("blk", "kv"),
            P("blk", "kv"),
            P("kv", "blk"),
            P("blk", "kv", None, None, None),
            P(),
            P(),
            P(),
        ),
        out_specs=(P(None, None, "blk"), P(None, "blk", "kv", None, None)),
        check_vma=False,
    )
```

```python
import functools
import math

import jax
import jax.numpy as jnp
from jax import lax
from jax.experimental import pallas as pl
from jax.experimental.pallas import tpu as pltpu
from jax.sharding import PartitionSpec as P

GROUP = 8


NEGATIVE = -1e30
EPSILON = 1e-05
ROPE_BASE = 5000000.0


MESH = pl.DeviceIdType.MESH


def remote(source, target, send, recv, axis, index):
    return pltpu.make_async_remote_copy(
        src_ref=source,
        dst_ref=target,
        send_sem=send,
        recv_sem=recv,
        device_id={axis: index},
        device_id_type=MESH,
    )


def kernel(
    sizes,
    slot_ref,
    embeds_ref,
    gain_ref,
    info_ref,
    cos_ref,
    sin_ref,
    wq_hbm,
    wk_hbm,
    wv_hbm,
    wo_hbm,
    cache_hbm,
    out_ref,
    appended_ref,
    weights,
    w_out,
    cache,
    stream,
    squares,
    part_a,
    part_b,
    sib_a,
    sib_b,
    z_a,
    z_b,
    turned,
    q_a,
    q_b,
    scores,
    seg_top,
    tops,
    ceilings,
    seg_num,
    seg_den,
    num,
    den,
    sib_num,
    sib_den,
    low_num,
    z_num,
    z_den,
    att_all,
    out_part,
    own_part,
    kv_part,
    out_rows,
    load_sem,
    sq_send,
    sq_recv,
    sib_send,
    sib_recv,
    z_send,
    z_recv,
    q_send,
    q_recv,
    top_send,
    top_recv,
    nsib_send,
    nsib_recv,
    nz_send,
    nz_recv,
    a_send,
    a_recv,
    kv_send,
    kv_recv,
    o_send,
    o_recv,
):
    n, kvn, steps, here, heads, hd, slots, width = sizes
    me = lax.axis_index("blk")
    kv = lax.axis_index("kv")
    chips = n // 2
    chip, core = me // 2, lax.rem(me, 2)
    sibling = me + 1 - 2 * core
    rows = steps * here
    beams = n * here
    quarter = n * rows // kvn
    half = heads // 2
    lanes = half * rows
    q_all = (q_a, q_b)
    parts, sib_parts, z_parts = (part_a, part_b), (sib_a, sib_b), (z_a, z_b)
    scaling = 1.0 / math.sqrt(hd)
    wide = w_out.shape[1]

    barrier = pltpu.get_barrier_semaphore()
    for d in range(1, n):
        pl.semaphore_signal(
            barrier, inc=1, device_id={"blk": lax.rem(me + d, n)}, device_id_type=MESH
        )
    for d in range(1, kvn):
        pl.semaphore_signal(
            barrier, inc=1, device_id={"kv": lax.rem(kv + d, kvn)}, device_id_type=MESH
        )
    hw = half * hd
    loads = [
        pltpu.make_async_copy(
            wq_hbm.at[:, pl.ds(0, hw)], weights.at[:, pl.ds(0, hw)], load_sem.at[0]
        ),
        pltpu.make_async_copy(wk_hbm, weights.at[:, pl.ds(hw, hd)], load_sem.at[1]),
        pltpu.make_async_copy(wv_hbm, weights.at[:, pl.ds(hw + hd, hd)], load_sem.at[2]),
        pltpu.make_async_copy(
            wq_hbm.at[:, pl.ds(hw, hw)], weights.at[:, pl.ds(hw + 2 * hd, hw)], load_sem.at[3]
        ),
        pltpu.make_async_copy(cache_hbm, cache, load_sem.at[4]),
        pltpu.make_async_copy(wo_hbm, w_out, load_sem.at[5]),
    ]
    for load in loads:
        load.start()

    x = embeds_ref[...].astype(jnp.float32)
    eye = lax.broadcasted_iota(jnp.int32, (beams, beams), 0) == lax.broadcasted_iota(
        jnp.int32, (beams, beams), 1
    )
    for s in range(steps):
        column = jnp.sum(x[s] * x[s], axis=1, keepdims=True)
        squares[0, s : s + 1, 0:beams] = jnp.sum(jnp.where(eye, column, 0.0), axis=0, keepdims=True)
    pl.semaphore_wait(barrier, n - 1 + kvn - 1)
    sends = []
    for d in range(1, n):
        sends.append(
            remote(
                squares.at[0], squares.at[d], sq_send.at[d], sq_recv.at[d], "blk", lax.rem(me + d, n)
            )
        )
        sends[-1].start()
    by_part = x.reshape(steps, n, here, wide).transpose(1, 0, 2, 3).reshape(n * rows, wide)
    stream[...] = by_part
    for send in sends:
        send.wait()
    normed = []
    for s in range(steps):
        total = squares[0, s : s + 1, 0:beams]
        for d in range(1, n):
            total = total + squares[d, s : s + 1, 0:beams]
        column = jnp.sum(jnp.where(eye, total, 0.0), axis=1, keepdims=True)
        normed.append(x[s] * lax.rsqrt(column / width + EPSILON) * gain_ref[...])
    normed = (
        jnp.stack(normed)
        .reshape(steps, chips, 2, here, wide)
        .transpose(2, 1, 0, 3, 4)
        .reshape(n * rows, wide)
        .astype(jnp.bfloat16)
    )
    for load in loads[:4]:
        load.wait()

    def across(source, target, send_sem, recv_sem):
        copies = []
        for d in range(1, chips):
            t = lax.rem(chip + d, chips)
            copies.append(
                remote(
                    source.at[t], target.at[d], send_sem.at[d], recv_sem.at[d], "blk", 2 * t + core
                )
            )
            copies[-1].start()
        return copies

    over = []
    first_column = 0
    for k in range(2):
        span = parts[k].shape[-1]
        parts[k][...] = jnp.dot(
            normed, weights[:, first_column : first_column + span], preferred_element_type=jnp.float32
        ).reshape(parts[k].shape)
        first_column += span
        over.append(
            remote(
                parts[k].at[1 - core], sib_parts[k], sib_send.at[k], sib_recv.at[k], "blk", sibling
            )
        )
        over[k].start()
    crossing = []
    for k in range(2):
        over[k].wait()
        sib_parts[k][...] = parts[k][core] + sib_parts[k][...]
        crossing.append(across(sib_parts[k], z_parts[k], z_send.at[k], z_recv.at[k]))
    loads[4].wait()

    def turn_values(i, carry):
        turned[i] = cache[i, 1].astype(jnp.float32).T.astype(jnp.bfloat16)
        return carry

    lax.fori_loop(0, slots, turn_values, 0, unroll=2)
    cos, sin = cos_ref[...], sin_ref[...]

    def rope(block):
        return block * cos + pltpu.roll(block, hd // 2, 1) * sin

    def arrived(k):
        for copy in crossing[k]:
            copy.wait()
        total = sib_parts[k][chip]
        for d in range(1, chips):
            total = total + z_parts[k][d]
        return total

    def spread(ref, send_sem, recv_sem):
        direct = []
        for d in range(1, chips):
            peer = 2 * lax.rem(chip + d, chips) + core
            direct.append(
                remote(ref.at[me], ref.at[me], send_sem.at[d], recv_sem.at[d], "blk", peer)
            )
            direct[-1].start()
        to_sibling = remote(
            ref.at[me], ref.at[me], send_sem.at[0], recv_sem.at[0], "blk", sibling
        )
        to_sibling.start()
        return direct, [to_sibling]

    def relay(ref, send_sem, recv_sem, copies):
        for d in range(1, chips):
            copies[0][d - 1].wait_recv()
            origin = 2 * lax.rem(chip + chips - d, chips) + core
            copies[1].append(
                remote(
                    ref.at[origin],
                    ref.at[origin],
                    send_sem.at[chips + d],
                    recv_sem.at[chips + d],
                    "blk",
                    sibling,
                )
            )
            copies[1][-1].start()

    def finish(copies):
        for copy in copies[1]:
            copy.wait()
        for copy in copies[0]:
            copy.wait_send()

    def turn_query(total):
        return jnp.concatenate(
            [rope(total[:, h * hd : (h + 1) * hd]) for h in range(half)], axis=0
        ).astype(jnp.bfloat16)

    queries, gathers = [None, None], [None, None]
    total = arrived(0)
    queries[0] = turn_query(total)
    q_all[0][me] = queries[0]
    gathers[0] = spread(q_all[0], q_send.at[0], q_recv.at[0])
    key = rope(total[:, half * hd : (half + 1) * hd]).astype(jnp.bfloat16)
    value_wide = total[:, (half + 1) * hd :]
    value = value_wide.astype(jnp.bfloat16)
    value_turned = value_wide.T.astype(jnp.bfloat16)
    entry = lax.broadcasted_iota(jnp.int32, (rows, lanes), 0)
    linked = jnp.zeros((rows, lanes), jnp.float32)
    for u in range(steps):
        seat = info_ref[me, 1 + u : 2 + u, :] + u * here
        known = info_ref[me, 1 + u : 2 + u, :] >= 0
        linked = jnp.where((entry == seat) & known, 1.0, linked)
    final = jnp.concatenate([linked[:, rows - here : rows]] * steps, axis=1)
    source = lax.broadcasted_iota(jnp.int32, (rows, rows), 0) // here
    wanted = lax.broadcasted_iota(jnp.int32, (rows, rows), 1) // here
    chosen = jnp.where(source == wanted, final, 0.0).T.astype(jnp.bfloat16)
    appended_ref[...] = jnp.dot(
        chosen, jnp.concatenate([key, value], axis=1), preferred_element_type=jnp.float32
    ).astype(jnp.bfloat16)
    queries[1] = turn_query(arrived(1))
    q_all[1][me] = queries[1]
    gathers[1] = spread(q_all[1], q_send.at[1], q_recv.at[1])
    relay(q_all[0], q_send.at[0], q_recv.at[0], gathers[0])

    contract_last = (((1,), (1,)), ((), ()))
    block = cache.shape[2]
    token = lax.broadcasted_iota(jnp.int32, (block, lanes), 0)
    own_scores, top_sends = [], []
    for k in range(2):
        own_scores.append(
            jnp.where(
                linked > 0,
                lax.dot_general(
                    key, queries[k], contract_last, preferred_element_type=jnp.float32
                )
                * scaling,
                NEGATIVE,
            )
        )
        own_top = jnp.max(own_scores[k], axis=0, keepdims=True)
        finish(gathers[k])

        def look(i, top):
            group = slot_ref[1 * slots + i]
            score = (
                lax.dot_general(
                    cache[slot_ref[i], 0],
                    q_all[k][group],
                    contract_last,
                    preferred_element_type=jnp.float32,
                )
                * scaling
            )
            limit = jnp.where(info_ref[group, 0:1, :] == slot_ref[2 * slots + i], slot_ref[3 * slots + i], 0)
            score = jnp.where(token < limit, score, NEGATIVE)
            scores[k, i] = score
            kept = jnp.where(slot_ref[4 * slots + i] > 0, top, NEGATIVE)
            top = jnp.maximum(kept, jnp.max(score, axis=0, keepdims=True))
            seg_top[i] = top
            return top

        lax.fori_loop(0, slots, look, jnp.full((1, lanes), NEGATIVE, jnp.float32), unroll=16)
        for g in range(n):
            top = jnp.where(slot_ref[5 * slots + n + g] > 0, seg_top[slot_ref[5 * slots + g]], NEGATIVE)
            tops[k, 0, g : g + 1, :] = jnp.where(me == g, jnp.maximum(top, own_top), top)
        copies = []
        for d in range(1, n):
            copies.append(
                remote(
                    tops.at[k, 0],
                    tops.at[k, d],
                    top_send.at[k, d],
                    top_recv.at[k, d],
                    "blk",
                    lax.rem(me + d, n),
                )
            )
            copies[-1].start()
        top_sends.append(copies)
        if k == 0:
            relay(q_all[1], q_send.at[1], q_recv.at[1], gathers[1])

    pairs, own_nums, own_dens = [], [], []

    def attend(k):
        for copy in top_sends[k]:
            copy.wait()
        ceiling = tops[k, 0]
        for d in range(1, n):
            ceiling = jnp.maximum(ceiling, tops[k, d])
        ceilings[...] = ceiling[:, None, :]

        def add(i, carry):
            total, count = carry
            probs = jnp.exp(scores[k, i] - ceilings[slot_ref[1 * slots + i]])
            same = slot_ref[4 * slots + i] > 0
            count = jnp.where(same, count, 0.0) + jnp.sum(probs, axis=0, keepdims=True)
            total = jnp.where(same, total, 0.0) + jnp.dot(
                turned[slot_ref[i]],
                probs.astype(jnp.bfloat16),
                preferred_element_type=jnp.float32,
            )
            seg_num[i] = total
            seg_den[i] = count
            return total, count

        lax.fori_loop(
            0,
            slots,
            add,
            (jnp.zeros((hd, lanes), jnp.float32), jnp.zeros((1, lanes), jnp.float32)),
            unroll=8,
        )
        own_probs = jnp.exp(own_scores[k] - ceilings[me])
        own_nums.append(
            jnp.dot(
                value_turned, own_probs.astype(jnp.bfloat16), preferred_element_type=jnp.float32
            ).T
        )
        own_dens.append(jnp.sum(own_probs, axis=0, keepdims=True))
        for t in range(chips):
            for c in range(2):
                g = 2 * t + c
                some = slot_ref[5 * slots + n + g] > 0
                num[k, c, t] = jnp.where(some, seg_num[slot_ref[5 * slots + g]], 0.0).T
                den[k, c, t] = jnp.where(some, seg_den[slot_ref[5 * slots + g]], 0.0)
        pair = [
            remote(
                num.at[k, 1 - core],
                sib_num.at[k],
                nsib_send.at[k, 0],
                nsib_recv.at[k, 0],
                "blk",
                sibling,
            ),
            remote(
                den.at[k, 1 - core],
                sib_den.at[k],
                nsib_send.at[k, 1],
                nsib_recv.at[k, 1],
                "blk",
                sibling,
            ),
        ]
        for copy in pair:
            copy.start()
        pairs.append(pair)

    def send_sums(k):
        for copy in pairs[k]:
            copy.wait()
        sib_num[k] = sib_num[k] + num[k, core]
        sib_den[k] = sib_den[k] + den[k, core]
        low_num[k] = sib_num[k].astype(jnp.bfloat16)
        return across(low_num.at[k], z_num.at[k], nz_send.at[k, 0], nz_recv.at[k, 0]) + across(
            sib_den.at[k], z_den.at[k], nz_send.at[k, 1], nz_recv.at[k, 1]
        )

    turn = lax.broadcasted_iota(jnp.int32, (lanes, lanes), 0) == lax.broadcasted_iota(
        jnp.int32, (lanes, lanes), 1
    )

    def close(k, copies):
        for copy in copies:
            copy.wait()
        numerator = own_nums[k] + sib_num[k, chip]
        denominator = own_dens[k] + sib_den[k, chip]
        for d in range(1, chips):
            numerator = numerator + z_num[k, d].astype(jnp.float32)
            denominator = denominator + z_den[k, d]
        column = jnp.sum(jnp.where(turn, denominator, 0.0), axis=1, keepdims=True)
        att_all[k, me] = (numerator / column).astype(jnp.bfloat16)
        return spread(att_all.at[k], a_send.at[k], a_recv.at[k])

    attend(0)
    sums = [send_sums(0)]
    attend(1)
    gathers = [close(0, sums[0])]
    sums.append(send_sums(1))
    relay(att_all.at[0], a_send.at[0], a_recv.at[0], gathers[0])
    gathers.append(close(1, sums[1]))
    loads[5].wait()

    def project(k):
        finish(gathers[k])
        attended = att_all[k].astype(jnp.float32).reshape(n, half, rows, hd)
        attended = jnp.concatenate(
            [attended[:, h].reshape(n * rows, hd) for h in range(half)], axis=1
        ).astype(jnp.bfloat16)
        return jnp.dot(
            attended,
            w_out[k * half * hd : (k + 1) * half * hd, :],
            preferred_element_type=jnp.float32,
        )

    early = project(0)
    relay(att_all.at[1], a_send.at[1], a_recv.at[1], gathers[1])
    out_sum = (early + project(1)).reshape(out_part.shape)
    out_part[...] = out_sum.astype(jnp.bfloat16)
    own_part[...] = out_sum
    sends = []
    for d in range(1, kvn):
        t = lax.rem(kv + d, kvn)
        sends.append(
            remote(out_part.at[t], kv_part.at[d], kv_send.at[d], kv_recv.at[d], "kv", t)
        )
        sends[-1].start()
    total = own_part[kv]
    for send in sends:
        send.wait()
    for d in range(1, kvn):
        total = total + kv_part[d].astype(jnp.float32)
    start = pl.multiple_of(kv * quarter, 16)
    out_rows[kv] = (stream[pl.ds(start, quarter)] + total).astype(jnp.bfloat16)
    sends = []
    for d in range(1, kvn):
        t = lax.rem(kv + d, kvn)
        sends.append(
            remote(out_rows.at[kv], out_rows.at[kv], o_send.at[d], o_recv.at[d], "kv", t)
        )
        sends[-1].start()
    for send in sends:
        send.wait()
    result = out_rows[...].astype(jnp.float32).reshape(n, steps, here, wide)
    out_ref[...] = result.transpose(1, 0, 2, 3).reshape(steps, beams, wide).astype(jnp.bfloat16)


def pick(table, index):
    count = table.shape[0]
    hit = index[:, None] == jnp.arange(count, dtype=jnp.int32)[None, :]
    return jnp.sum(jnp.where(hit, table[None, :], 0), axis=1)


def body(
    embeds, attn_gain, w_query, w_key, w_value, w_out, cache_kv, lengths, block_table, parents
):
    n = lax.axis_size("blk")
    kvn = lax.axis_size("kv")
    shard = lax.axis_index("blk")
    steps, beams, wide = embeds.shape
    here = beams // n
    slots = cache_kv.shape[0]
    block, hd = cache_kv.shape[3], cache_kv.shape[4]
    heads = w_query.shape[1] // hd
    rows = here * steps
    half = heads // 2
    lanes = half * rows
    all_beams = jnp.arange(beams, dtype=jnp.int32)
    roots, origin = [], []
    for s in range(steps):
        before = roots[-1] if s else all_beams
        roots.append(pick(before, parents[s]))
        origin.append([pick(line, parents[s]) for line in (origin[-1] if s else [])] + [all_beams])
    root = jnp.stack(roots)
    slot_ids = shard * slots + jnp.arange(slots, dtype=jnp.int32)
    named = block_table[None] == slot_ids[:, None, None]
    code = jnp.arange(block_table.size, dtype=jnp.int32).reshape(block_table.shape) + 1
    code = jnp.sum(jnp.where(named, code[None], 0), axis=(1, 2)) - 1
    filled = code >= 0
    owner = jnp.where(filled, code // block_table.shape[1], -1)
    logical = code % block_table.shape[1]
    tokens = jnp.where(filled, pick(lengths, jnp.maximum(owner, 0)) - logical * block, 0)
    group = jnp.where(filled, owner // GROUP, n - 1)
    place = jnp.arange(slots, dtype=jnp.int32)
    before = (group[None, :] == group[:, None]) & (place[None, :] < place[:, None])
    rank = jnp.sum((group[None, :] < group[:, None]) | before, axis=1)
    same = jnp.sum(before, axis=1)
    table = jnp.stack([place, group, owner, tokens, same.astype(jnp.int32)])
    table = jnp.sum(jnp.where((rank[:, None] == place[None, :])[None], table[:, :, None], 0), axis=1)
    every = jnp.arange(n, dtype=jnp.int32)[:, None]
    upto = jnp.sum(group[None, :] <= every, axis=1)
    held = jnp.sum(group[None, :] == every, axis=1)
    table = jnp.concatenate(
        [table.reshape(-1), jnp.maximum(upto - 1, 0), held], dtype=jnp.int32
    )
    base = all_beams // here * here
    info = jnp.stack(
        [
            jnp.stack([roots[s] if u < 0 else origin[s][u] - base if u <= s else base * 0 - 1
                       for s in range(steps)])
            for u in range(-1, steps)
        ]
    )
    info = info.reshape(1 + steps, steps, n, here).transpose(2, 0, 1, 3).reshape(n, 1 + steps, 1, rows)
    info = jnp.broadcast_to(info, (n, 1 + steps, half, rows)).reshape(n, 1 + steps, lanes)
    own = lax.dynamic_slice_in_dim(root, shard * here, here, 1)
    position = pick(lengths, own.reshape(-1)).reshape(steps, here) + jnp.arange(
        steps, dtype=jnp.int32
    )[:, None]
    lane = jnp.arange(hd, dtype=jnp.int32)
    exponent = (lane % (hd // 2)).astype(jnp.float32) * (2.0 / hd)
    angles = position.reshape(rows).astype(jnp.float32)[:, None] * (ROPE_BASE ** (-exponent))
    cos = jnp.cos(angles)
    sin = jnp.sin(angles) * jnp.where(lane < hd // 2, -1.0, 1.0)

    chips = n // 2
    total_rows = n * rows
    columns = (heads + 2) * hd
    quarter = total_rows // kvn
    sizes = (n, kvn, steps, here, heads, hd, slots, wide * n)
    bf16, f32 = jnp.bfloat16, jnp.float32
    dma = pltpu.SemaphoreType.DMA
    lane_room = -(-beams // 128) * 128
    vmem = pl.BlockSpec(memory_space=pltpu.VMEM)
    smem = pl.BlockSpec(memory_space=pltpu.SMEM)
    hbm = pl.BlockSpec(memory_space=pl.ANY)
    out, appended = pl.pallas_call(
        functools.partial(kernel, sizes),
        out_shape=(
            jax.ShapeDtypeStruct((steps, beams, wide), bf16),
            jax.ShapeDtypeStruct((rows, 2 * hd), bf16),
        ),
        in_specs=[smem] + [vmem] * 5 + [hbm] * 5,
        out_specs=(vmem, vmem),
        scratch_shapes=[
            pltpu.VMEM((wide, columns), bf16),
            pltpu.VMEM((heads * hd, wide), bf16),
            pltpu.VMEM((slots, 2, block, hd), bf16),
            pltpu.VMEM((total_rows, wide), f32),
            pltpu.VMEM((n, 8, lane_room), f32),
            pltpu.VMEM((2, chips, rows, (half + 2) * hd), f32),
            pltpu.VMEM((2, chips, rows, half * hd), f32),
            pltpu.VMEM((chips, rows, (half + 2) * hd), f32),
            pltpu.VMEM((chips, rows, half * hd), f32),
            pltpu.VMEM((chips, rows, (half + 2) * hd), f32),
            pltpu.VMEM((chips, rows, half * hd), f32),
            pltpu.VMEM((slots, hd, block), bf16),
            pltpu.VMEM((n, lanes, hd), bf16),
            pltpu.VMEM((n, lanes, hd), bf16),
            pltpu.VMEM((2, slots, block, lanes), f32),
            pltpu.VMEM((slots, 1, lanes), f32),
            pltpu.VMEM((2, n, n, lanes), f32),
            pltpu.VMEM((n, 1, lanes), f32),
            pltpu.VMEM((slots, hd, lanes), f32),
            pltpu.VMEM((slots, 1, lanes), f32),
            pltpu.VMEM((2, 2, chips, lanes, hd), f32),
            pltpu.VMEM((2, 2, chips, 1, lanes), f32),
            pltpu.VMEM((2, chips, lanes, hd), f32),
            pltpu.VMEM((2, chips, 1, lanes), f32),
            pltpu.VMEM((2, chips, lanes, hd), bf16),
            pltpu.VMEM((2, chips, lanes, hd), bf16),
            pltpu.VMEM((2, chips, 1, lanes), f32),
            pltpu.VMEM((2, n, lanes, hd), bf16),
            pltpu.VMEM((kvn, quarter, wide), bf16),
            pltpu.VMEM((kvn, quarter, wide), f32),
            pltpu.VMEM((kvn, quarter, wide), bf16),
            pltpu.VMEM((kvn, quarter, wide), bf16),
            dma((6,)),
            dma((n,)),
            dma((n,)),
            dma((2,)),
            dma((2,)),
            dma((2, chips)),
            dma((2, chips)),
            dma((2, n)),
            dma((2, n)),
            dma((2, n)),
            dma((2, n)),
            dma((2, 2)),
            dma((2, 2)),
            dma((2, 2, chips)),
            dma((2, 2, chips)),
            dma((2, n)),
            dma((2, n)),
            dma((kvn,)),
            dma((kvn,)),
            dma((kvn,)),
            dma((kvn,)),
        ],
        compiler_params=pltpu.CompilerParams(
            collective_id=0, has_side_effects=True, vmem_limit_bytes=60 * 1024 * 1024
        ),
    )(
        table,
        embeds,
        attn_gain[None, :],
        info,
        cos,
        sin,
        w_query,
        w_key,
        w_value,
        w_out,
        cache_kv.reshape(slots, 2, block, hd),
    )
    return out, appended.reshape(steps, here, 1, 2, hd)


def solution(mesh):
    return jax.shard_map(
        body,
        mesh=mesh,
        in_specs=(
            P(None, None, "blk"),
            P("blk"),
            P("blk", "kv"),
            P("blk", "kv"),
            P("blk", "kv"),
            P("kv", "blk"),
            P("blk", "kv", None, None, None),
            P(),
            P(),
            P(),
        ),
        out_specs=(P(None, None, "blk"), P(None, "blk", "kv", None, None)),
        check_vma=False,
    )
```

```python
import functools
import math

import jax
import jax.numpy as jnp
from jax import lax
from jax.experimental import pallas as pl
from jax.experimental.pallas import tpu as pltpu
from jax.sharding import PartitionSpec as P

GROUP = 8


NEGATIVE = -1e30
EPSILON = 1e-05
ROPE_BASE = 5000000.0


MESH = pl.DeviceIdType.MESH


def remote(source, target, send, recv, axis, index):
    return pltpu.make_async_remote_copy(
        src_ref=source,
        dst_ref=target,
        send_sem=send,
        recv_sem=recv,
        device_id={axis: index},
        device_id_type=MESH,
    )


def kernel(
    sizes,
    slot_ref,
    embeds_ref,
    gain_ref,
    info_ref,
    cos_ref,
    sin_ref,
    wq_hbm,
    wk_hbm,
    wv_hbm,
    wo_hbm,
    cache_hbm,
    out_ref,
    appended_ref,
    weights,
    w_out,
    cache,
    stream,
    squares,
    part_a,
    part_b,
    sib_a,
    sib_b,
    z_a,
    z_b,
    turned,
    q_a,
    q_b,
    scores,
    seg_top,
    tops,
    ceilings,
    seg_num,
    seg_den,
    num,
    den,
    sib_num,
    sib_den,
    low_num,
    z_num,
    z_den,
    att_all,
    out_part,
    own_part,
    kv_part,
    out_rows,
    load_sem,
    sq_send,
    sq_recv,
    sib_send,
    sib_recv,
    z_send,
    z_recv,
    q_send,
    q_recv,
    top_send,
    top_recv,
    nsib_send,
    nsib_recv,
    nz_send,
    nz_recv,
    a_send,
    a_recv,
    kv_send,
    kv_recv,
    o_send,
    o_recv,
):
    n, kvn, steps, here, heads, hd, slots, width = sizes
    me = lax.axis_index("blk")
    kv = lax.axis_index("kv")
    chips = n // 2
    chip, core = me // 2, lax.rem(me, 2)
    sibling = me + 1 - 2 * core
    rows = steps * here
    beams = n * here
    quarter = n * rows // kvn
    half = heads // 2
    lanes = half * rows
    q_all = (q_a, q_b)
    parts, sib_parts, z_parts = (part_a, part_b), (sib_a, sib_b), (z_a, z_b)
    scaling = 1.0 / math.sqrt(hd)
    wide = w_out.shape[1]

    barrier = pltpu.get_barrier_semaphore()
    for d in range(1, n):
        pl.semaphore_signal(
            barrier, inc=1, device_id={"blk": lax.rem(me + d, n)}, device_id_type=MESH
        )
    for d in range(1, kvn):
        pl.semaphore_signal(
            barrier, inc=1, device_id={"kv": lax.rem(kv + d, kvn)}, device_id_type=MESH
        )
    hw = half * hd
    loads = [
        pltpu.make_async_copy(
            wq_hbm.at[:, pl.ds(0, hw)], weights.at[:, pl.ds(0, hw)], load_sem.at[0]
        ),
        pltpu.make_async_copy(wk_hbm, weights.at[:, pl.ds(hw, hd)], load_sem.at[1]),
        pltpu.make_async_copy(wv_hbm, weights.at[:, pl.ds(hw + hd, hd)], load_sem.at[2]),
        pltpu.make_async_copy(
            wq_hbm.at[:, pl.ds(hw, hw)], weights.at[:, pl.ds(hw + 2 * hd, hw)], load_sem.at[3]
        ),
        pltpu.make_async_copy(cache_hbm, cache, load_sem.at[4]),
        pltpu.make_async_copy(wo_hbm, w_out, load_sem.at[5]),
    ]
    for load in loads:
        load.start()

    x = embeds_ref[...].astype(jnp.float32)
    eye = lax.broadcasted_iota(jnp.int32, (beams, beams), 0) == lax.broadcasted_iota(
        jnp.int32, (beams, beams), 1
    )
    for s in range(steps):
        column = jnp.sum(x[s] * x[s], axis=1, keepdims=True)
        squares[0, s : s + 1, 0:beams] = jnp.sum(jnp.where(eye, column, 0.0), axis=0, keepdims=True)
    pl.semaphore_wait(barrier, n - 1 + kvn - 1)
    sends = []
    for d in range(1, n):
        sends.append(
            remote(
                squares.at[0], squares.at[d], sq_send.at[d], sq_recv.at[d], "blk", lax.rem(me + d, n)
            )
        )
        sends[-1].start()
    by_part = x.reshape(steps, n, here, wide).transpose(1, 0, 2, 3).reshape(n * rows, wide)
    stream[...] = by_part
    for send in sends:
        send.wait()
    normed = []
    for s in range(steps):
        total = squares[0, s : s + 1, 0:beams]
        for d in range(1, n):
            total = total + squares[d, s : s + 1, 0:beams]
        column = jnp.sum(jnp.where(eye, total, 0.0), axis=1, keepdims=True)
        normed.append(x[s] * lax.rsqrt(column / width + EPSILON) * gain_ref[...])
    normed = (
        jnp.stack(normed)
        .reshape(steps, chips, 2, here, wide)
        .transpose(2, 1, 0, 3, 4)
        .reshape(n * rows, wide)
        .astype(jnp.bfloat16)
    )
    for load in loads[:4]:
        load.wait()

    def across(source, target, send_sem, recv_sem):
        copies = []
        for d in range(1, chips):
            t = lax.rem(chip + d, chips)
            copies.append(
                remote(
                    source.at[t], target.at[d], send_sem.at[d], recv_sem.at[d], "blk", 2 * t + core
                )
            )
            copies[-1].start()
        return copies

    over = []
    first_column = 0
    for k in range(2):
        span = parts[k].shape[-1]
        parts[k][...] = jnp.dot(
            normed, weights[:, first_column : first_column + span], preferred_element_type=jnp.float32
        ).reshape(parts[k].shape)
        first_column += span
        over.append(
            remote(
                parts[k].at[1 - core], sib_parts[k], sib_send.at[k], sib_recv.at[k], "blk", sibling
            )
        )
        over[k].start()
    crossing = []
    for k in range(2):
        over[k].wait()
        sib_parts[k][...] = parts[k][core] + sib_parts[k][...]
        crossing.append(across(sib_parts[k], z_parts[k], z_send.at[k], z_recv.at[k]))
    loads[4].wait()

    def turn_values(i, carry):
        turned[i] = cache[i, 1].astype(jnp.float32).T.astype(jnp.bfloat16)
        return carry

    lax.fori_loop(0, slots, turn_values, 0, unroll=2)
    cos, sin = cos_ref[...], sin_ref[...]

    def rope(block):
        return block * cos + pltpu.roll(block, hd // 2, 1) * sin

    def arrived(k):
        for copy in crossing[k]:
            copy.wait()
        total = sib_parts[k][chip]
        for d in range(1, chips):
            total = total + z_parts[k][d]
        return total

    def spread(ref, send_sem, recv_sem):
        direct = []
        for d in range(1, chips):
            peer = 2 * lax.rem(chip + d, chips) + core
            direct.append(
                remote(ref.at[me], ref.at[me], send_sem.at[d], recv_sem.at[d], "blk", peer)
            )
            direct[-1].start()
        to_sibling = remote(
            ref.at[me], ref.at[me], send_sem.at[0], recv_sem.at[0], "blk", sibling
        )
        to_sibling.start()
        return direct, [to_sibling]

    def relay(ref, send_sem, recv_sem, copies):
        for d in range(1, chips):
            copies[0][d - 1].wait_recv()
            origin = 2 * lax.rem(chip + chips - d, chips) + core
            copies[1].append(
                remote(
                    ref.at[origin],
                    ref.at[origin],
                    send_sem.at[chips + d],
                    recv_sem.at[chips + d],
                    "blk",
                    sibling,
                )
            )
            copies[1][-1].start()

    def finish(copies):
        for copy in copies[1]:
            copy.wait()
        for copy in copies[0]:
            copy.wait_send()

    def turn_query(total):
        return jnp.concatenate(
            [rope(total[:, h * hd : (h + 1) * hd]) for h in range(half)], axis=0
        ).astype(jnp.bfloat16)

    queries, gathers = [None, None], [None, None]
    total = arrived(0)
    queries[0] = turn_query(total)
    q_all[0][me] = queries[0]
    gathers[0] = spread(q_all[0], q_send.at[0], q_recv.at[0])
    key = rope(total[:, half * hd : (half + 1) * hd]).astype(jnp.bfloat16)
    value_wide = total[:, (half + 1) * hd :]
    value = value_wide.astype(jnp.bfloat16)
    value_turned = value_wide.T.astype(jnp.bfloat16)
    entry = lax.broadcasted_iota(jnp.int32, (rows, lanes), 0)
    linked = jnp.zeros((rows, lanes), jnp.float32)
    for u in range(steps):
        seat = info_ref[me, 1 + u : 2 + u, :] + u * here
        known = info_ref[me, 1 + u : 2 + u, :] >= 0
        linked = jnp.where((entry == seat) & known, 1.0, linked)
    final = jnp.concatenate([linked[:, rows - here : rows]] * steps, axis=1)
    source = lax.broadcasted_iota(jnp.int32, (rows, rows), 0) // here
    wanted = lax.broadcasted_iota(jnp.int32, (rows, rows), 1) // here
    chosen = jnp.where(source == wanted, final, 0.0).T.astype(jnp.bfloat16)
    appended_ref[...] = jnp.dot(
        chosen, jnp.concatenate([key, value], axis=1), preferred_element_type=jnp.float32
    ).astype(jnp.bfloat16)
    queries[1] = turn_query(arrived(1))
    q_all[1][me] = queries[1]
    gathers[1] = spread(q_all[1], q_send.at[1], q_recv.at[1])
    relay(q_all[0], q_send.at[0], q_recv.at[0], gathers[0])

    contract_last = (((1,), (1,)), ((), ()))
    block = cache.shape[2]
    token = lax.broadcasted_iota(jnp.int32, (block, lanes), 0)
    own_scores, top_sends = [], []
    for k in range(2):
        own_scores.append(
            jnp.where(
                linked > 0,
                lax.dot_general(
                    key, queries[k], contract_last, preferred_element_type=jnp.float32
                )
                * scaling,
                NEGATIVE,
            )
        )
        own_top = jnp.max(own_scores[k], axis=0, keepdims=True)
        finish(gathers[k])

        def look(i, top):
            group = slot_ref[1 * slots + i]
            score = (
                lax.dot_general(
                    cache[slot_ref[i], 0],
                    q_all[k][group],
                    contract_last,
                    preferred_element_type=jnp.float32,
                )
                * scaling
            )
            limit = jnp.where(info_ref[group, 0:1, :] == slot_ref[2 * slots + i], slot_ref[3 * slots + i], 0)
            score = jnp.where(token < limit, score, NEGATIVE)
            scores[k, i] = score
            kept = jnp.where(slot_ref[4 * slots + i] > 0, top, NEGATIVE)
            top = jnp.maximum(kept, jnp.max(score, axis=0, keepdims=True))
            seg_top[i] = top
            return top

        top = lax.fori_loop(
            0, slots // 2, look, jnp.full((1, lanes), NEGATIVE, jnp.float32), unroll=16
        )
        if k == 0:
            relay(q_all[1], q_send.at[1], q_recv.at[1], gathers[1])
        lax.fori_loop(slots // 2, slots, look, top, unroll=16)
        for g in range(n):
            top = jnp.where(slot_ref[5 * slots + n + g] > 0, seg_top[slot_ref[5 * slots + g]], NEGATIVE)
            tops[k, 0, g : g + 1, :] = jnp.where(me == g, jnp.maximum(top, own_top), top)
        copies = []
        for d in range(1, n):
            copies.append(
                remote(
                    tops.at[k, 0],
                    tops.at[k, d],
                    top_send.at[k, d],
                    top_recv.at[k, d],
                    "blk",
                    lax.rem(me + d, n),
                )
            )
            copies[-1].start()
        top_sends.append(copies)

    pairs, own_nums, own_dens = [], [], []

    def attend(k, between):
        for copy in top_sends[k]:
            copy.wait()
        ceiling = tops[k, 0]
        for d in range(1, n):
            ceiling = jnp.maximum(ceiling, tops[k, d])
        ceilings[...] = ceiling[:, None, :]

        def add(i, carry):
            total, count = carry
            probs = jnp.exp(scores[k, i] - ceilings[slot_ref[1 * slots + i]])
            same = slot_ref[4 * slots + i] > 0
            count = jnp.where(same, count, 0.0) + jnp.sum(probs, axis=0, keepdims=True)
            total = jnp.where(same, total, 0.0) + jnp.dot(
                turned[slot_ref[i]],
                probs.astype(jnp.bfloat16),
                preferred_element_type=jnp.float32,
            )
            seg_num[i] = total
            seg_den[i] = count
            return total, count

        carry = lax.fori_loop(
            0,
            slots // 2,
            add,
            (jnp.zeros((hd, lanes), jnp.float32), jnp.zeros((1, lanes), jnp.float32)),
            unroll=8,
        )
        between()
        lax.fori_loop(slots // 2, slots, add, carry, unroll=8)
        own_probs = jnp.exp(own_scores[k] - ceilings[me])
        own_nums.append(
            jnp.dot(
                value_turned, own_probs.astype(jnp.bfloat16), preferred_element_type=jnp.float32
            ).T
        )
        own_dens.append(jnp.sum(own_probs, axis=0, keepdims=True))
        for t in range(chips):
            for c in range(2):
                g = 2 * t + c
                some = slot_ref[5 * slots + n + g] > 0
                num[k, c, t] = jnp.where(some, seg_num[slot_ref[5 * slots + g]], 0.0).T
                den[k, c, t] = jnp.where(some, seg_den[slot_ref[5 * slots + g]], 0.0)
        pair = [
            remote(
                num.at[k, 1 - core],
                sib_num.at[k],
                nsib_send.at[k, 0],
                nsib_recv.at[k, 0],
                "blk",
                sibling,
            ),
            remote(
                den.at[k, 1 - core],
                sib_den.at[k],
                nsib_send.at[k, 1],
                nsib_recv.at[k, 1],
                "blk",
                sibling,
            ),
        ]
        for copy in pair:
            copy.start()
        pairs.append(pair)

    def send_sums(k):
        for copy in pairs[k]:
            copy.wait()
        sib_num[k] = sib_num[k] + num[k, core]
        sib_den[k] = sib_den[k] + den[k, core]
        low_num[k] = sib_num[k].astype(jnp.bfloat16)
        return across(low_num.at[k], z_num.at[k], nz_send.at[k, 0], nz_recv.at[k, 0]) + across(
            sib_den.at[k], z_den.at[k], nz_send.at[k, 1], nz_recv.at[k, 1]
        )

    turn = lax.broadcasted_iota(jnp.int32, (lanes, lanes), 0) == lax.broadcasted_iota(
        jnp.int32, (lanes, lanes), 1
    )

    def close(k, copies):
        for copy in copies:
            copy.wait()
        numerator = own_nums[k] + sib_num[k, chip]
        denominator = own_dens[k] + sib_den[k, chip]
        for d in range(1, chips):
            numerator = numerator + z_num[k, d].astype(jnp.float32)
            denominator = denominator + z_den[k, d]
        column = jnp.sum(jnp.where(turn, denominator, 0.0), axis=1, keepdims=True)
        att_all[k, me] = (numerator / column).astype(jnp.bfloat16)
        return spread(att_all.at[k], a_send.at[k], a_recv.at[k])

    sums = []
    attend(0, lambda: None)
    attend(1, lambda: sums.append(send_sums(0)))
    gathers = [close(0, sums[0])]
    sums.append(send_sums(1))
    relay(att_all.at[0], a_send.at[0], a_recv.at[0], gathers[0])
    gathers.append(close(1, sums[1]))
    loads[5].wait()

    def gathered(k):
        finish(gathers[k])
        attended = att_all[k].astype(jnp.float32).reshape(n, half, rows, hd)
        return jnp.concatenate(
            [attended[:, h].reshape(n * rows, hd) for h in range(half)], axis=1
        ).astype(jnp.bfloat16)

    early = jnp.dot(gathered(0), w_out[0:hw, :], preferred_element_type=jnp.float32)
    relay(att_all.at[1], a_send.at[1], a_recv.at[1], gathers[1])
    late = gathered(1)
    pieces = out_rows.shape[0]
    span = wide // pieces
    rounds = []
    for c in range(pieces):
        piece = early[:, c * span : (c + 1) * span] + jnp.dot(
            late,
            w_out[hw : 2 * hw, c * span : (c + 1) * span],
            preferred_element_type=jnp.float32,
        )
        own_part[c] = piece.reshape(kvn, quarter, span)
        out_part[c] = own_part[c].astype(jnp.bfloat16)
        sends = []
        for d in range(1, kvn):
            t = lax.rem(kv + d, kvn)
            sends.append(
                remote(
                    out_part.at[c, t],
                    kv_part.at[c, d],
                    kv_send.at[c, d],
                    kv_recv.at[c, d],
                    "kv",
                    t,
                )
            )
            sends[-1].start()
        rounds.append(sends)
    start = pl.multiple_of(kv * quarter, 16)
    finals = []
    for c in range(pieces):
        for send in rounds[c]:
            send.wait()
        total = own_part[c, kv]
        for d in range(1, kvn):
            total = total + kv_part[c, d].astype(jnp.float32)
        residual = stream[pl.ds(start, quarter), c * span : (c + 1) * span]
        out_rows[c, kv] = (residual + total).astype(jnp.bfloat16)
        for d in range(1, kvn):
            t = lax.rem(kv + d, kvn)
            finals.append(
                remote(
                    out_rows.at[c, kv],
                    out_rows.at[c, kv],
                    o_send.at[c, d],
                    o_recv.at[c, d],
                    "kv",
                    t,
                )
            )
            finals[-1].start()
    for send in finals:
        send.wait()
    for c in range(pieces):
        result = out_rows[c].astype(jnp.float32).reshape(n, steps, here, span)
        out_ref[:, :, c * span : (c + 1) * span] = (
            result.transpose(1, 0, 2, 3).reshape(steps, beams, span).astype(jnp.bfloat16)
        )


def pick(table, index):
    count = table.shape[0]
    hit = index[:, None] == jnp.arange(count, dtype=jnp.int32)[None, :]
    return jnp.sum(jnp.where(hit, table[None, :], 0), axis=1)


def body(
    embeds, attn_gain, w_query, w_key, w_value, w_out, cache_kv, lengths, block_table, parents
):
    n = lax.axis_size("blk")
    kvn = lax.axis_size("kv")
    shard = lax.axis_index("blk")
    steps, beams, wide = embeds.shape
    here = beams // n
    slots = cache_kv.shape[0]
    block, hd = cache_kv.shape[3], cache_kv.shape[4]
    heads = w_query.shape[1] // hd
    rows = here * steps
    half = heads // 2
    lanes = half * rows
    all_beams = jnp.arange(beams, dtype=jnp.int32)
    roots, origin = [], []
    for s in range(steps):
        before = roots[-1] if s else all_beams
        roots.append(pick(before, parents[s]))
        origin.append([pick(line, parents[s]) for line in (origin[-1] if s else [])] + [all_beams])
    root = jnp.stack(roots)
    slot_ids = shard * slots + jnp.arange(slots, dtype=jnp.int32)
    named = block_table[None] == slot_ids[:, None, None]
    code = jnp.arange(block_table.size, dtype=jnp.int32).reshape(block_table.shape) + 1
    code = jnp.sum(jnp.where(named, code[None], 0), axis=(1, 2)) - 1
    filled = code >= 0
    owner = jnp.where(filled, code // block_table.shape[1], -1)
    logical = code % block_table.shape[1]
    tokens = jnp.where(filled, pick(lengths, jnp.maximum(owner, 0)) - logical * block, 0)
    group = jnp.where(filled, owner // GROUP, n - 1)
    place = jnp.arange(slots, dtype=jnp.int32)
    before = (group[None, :] == group[:, None]) & (place[None, :] < place[:, None])
    rank = jnp.sum((group[None, :] < group[:, None]) | before, axis=1)
    same = jnp.sum(before, axis=1)
    table = jnp.stack([place, group, owner, tokens, same.astype(jnp.int32)])
    table = jnp.sum(jnp.where((rank[:, None] == place[None, :])[None], table[:, :, None], 0), axis=1)
    every = jnp.arange(n, dtype=jnp.int32)[:, None]
    upto = jnp.sum(group[None, :] <= every, axis=1)
    held = jnp.sum(group[None, :] == every, axis=1)
    table = jnp.concatenate(
        [table.reshape(-1), jnp.maximum(upto - 1, 0), held], dtype=jnp.int32
    )
    base = all_beams // here * here
    info = jnp.stack(
        [
            jnp.stack([roots[s] if u < 0 else origin[s][u] - base if u <= s else base * 0 - 1
                       for s in range(steps)])
            for u in range(-1, steps)
        ]
    )
    info = info.reshape(1 + steps, steps, n, here).transpose(2, 0, 1, 3).reshape(n, 1 + steps, 1, rows)
    info = jnp.broadcast_to(info, (n, 1 + steps, half, rows)).reshape(n, 1 + steps, lanes)
    own = lax.dynamic_slice_in_dim(root, shard * here, here, 1)
    position = pick(lengths, own.reshape(-1)).reshape(steps, here) + jnp.arange(
        steps, dtype=jnp.int32
    )[:, None]
    lane = jnp.arange(hd, dtype=jnp.int32)
    exponent = (lane % (hd // 2)).astype(jnp.float32) * (2.0 / hd)
    angles = position.reshape(rows).astype(jnp.float32)[:, None] * (ROPE_BASE ** (-exponent))
    cos = jnp.cos(angles)
    sin = jnp.sin(angles) * jnp.where(lane < hd // 2, -1.0, 1.0)

    chips = n // 2
    total_rows = n * rows
    columns = (heads + 2) * hd
    quarter = total_rows // kvn
    pieces = 2 if wide % 256 == 0 else 1
    sizes = (n, kvn, steps, here, heads, hd, slots, wide * n)
    bf16, f32 = jnp.bfloat16, jnp.float32
    dma = pltpu.SemaphoreType.DMA
    lane_room = -(-beams // 128) * 128
    vmem = pl.BlockSpec(memory_space=pltpu.VMEM)
    smem = pl.BlockSpec(memory_space=pltpu.SMEM)
    hbm = pl.BlockSpec(memory_space=pl.ANY)
    out, appended = pl.pallas_call(
        functools.partial(kernel, sizes),
        out_shape=(
            jax.ShapeDtypeStruct((steps, beams, wide), bf16),
            jax.ShapeDtypeStruct((rows, 2 * hd), bf16),
        ),
        in_specs=[smem] + [vmem] * 5 + [hbm] * 5,
        out_specs=(vmem, vmem),
        scratch_shapes=[
            pltpu.VMEM((wide, columns), bf16),
            pltpu.VMEM((heads * hd, wide), bf16),
            pltpu.VMEM((slots, 2, block, hd), bf16),
            pltpu.VMEM((total_rows, wide), f32),
            pltpu.VMEM((n, 8, lane_room), f32),
            pltpu.VMEM((2, chips, rows, (half + 2) * hd), f32),
            pltpu.VMEM((2, chips, rows, half * hd), f32),
            pltpu.VMEM((chips, rows, (half + 2) * hd), f32),
            pltpu.VMEM((chips, rows, half * hd), f32),
            pltpu.VMEM((chips, rows, (half + 2) * hd), f32),
            pltpu.VMEM((chips, rows, half * hd), f32),
            pltpu.VMEM((slots, hd, block), bf16),
            pltpu.VMEM((n, lanes, hd), bf16),
            pltpu.VMEM((n, lanes, hd), bf16),
            pltpu.VMEM((2, slots, block, lanes), f32),
            pltpu.VMEM((slots, 1, lanes), f32),
            pltpu.VMEM((2, n, n, lanes), f32),
            pltpu.VMEM((n, 1, lanes), f32),
            pltpu.VMEM((slots, hd, lanes), f32),
            pltpu.VMEM((slots, 1, lanes), f32),
            pltpu.VMEM((2, 2, chips, lanes, hd), f32),
            pltpu.VMEM((2, 2, chips, 1, lanes), f32),
            pltpu.VMEM((2, chips, lanes, hd), f32),
            pltpu.VMEM((2, chips, 1, lanes), f32),
            pltpu.VMEM((2, chips, lanes, hd), bf16),
            pltpu.VMEM((2, chips, lanes, hd), bf16),
            pltpu.VMEM((2, chips, 1, lanes), f32),
            pltpu.VMEM((2, n, lanes, hd), bf16),
            pltpu.VMEM((pieces, kvn, quarter, wide // pieces), bf16),
            pltpu.VMEM((pieces, kvn, quarter, wide // pieces), f32),
            pltpu.VMEM((pieces, kvn, quarter, wide // pieces), bf16),
            pltpu.VMEM((pieces, kvn, quarter, wide // pieces), bf16),
            dma((6,)),
            dma((n,)),
            dma((n,)),
            dma((2,)),
            dma((2,)),
            dma((2, chips)),
            dma((2, chips)),
            dma((2, n)),
            dma((2, n)),
            dma((2, n)),
            dma((2, n)),
            dma((2, 2)),
            dma((2, 2)),
            dma((2, 2, chips)),
            dma((2, 2, chips)),
            dma((2, n)),
            dma((2, n)),
            dma((pieces, kvn)),
            dma((pieces, kvn)),
            dma((pieces, kvn)),
            dma((pieces, kvn)),
        ],
        compiler_params=pltpu.CompilerParams(
            collective_id=0, has_side_effects=True, vmem_limit_bytes=60 * 1024 * 1024
        ),
    )(
        table,
        embeds,
        attn_gain[None, :],
        info,
        cos,
        sin,
        w_query,
        w_key,
        w_value,
        w_out,
        cache_kv.reshape(slots, 2, block, hd),
    )
    return out, appended.reshape(steps, here, 1, 2, hd)


def solution(mesh):
    return jax.shard_map(
        body,
        mesh=mesh,
        in_specs=(
            P(None, None, "blk"),
            P("blk"),
            P("blk", "kv"),
            P("blk", "kv"),
            P("blk", "kv"),
            P("kv", "blk"),
            P("blk", "kv", None, None, None),
            P(),
            P(),
            P(),
        ),
        out_specs=(P(None, None, "blk"), P(None, "blk", "kv", None, None)),
        check_vma=False,
    )
```

```python
import functools
import math

import jax
import jax.numpy as jnp
from jax import lax
from jax.experimental import pallas as pl
from jax.experimental.pallas import tpu as pltpu
from jax.sharding import PartitionSpec as P

GROUP = 8


NEGATIVE = -1e30
EPSILON = 1e-05
ROPE_BASE = 5000000.0


MESH = pl.DeviceIdType.MESH


def remote(source, target, send, recv, axis, index):
    return pltpu.make_async_remote_copy(
        src_ref=source,
        dst_ref=target,
        send_sem=send,
        recv_sem=recv,
        device_id={axis: index},
        device_id_type=MESH,
    )


def kernel(
    sizes,
    slot_ref,
    embeds_ref,
    gain_ref,
    info_ref,
    cos_ref,
    sin_ref,
    wq_hbm,
    wk_hbm,
    wv_hbm,
    wo_hbm,
    cache_hbm,
    out_ref,
    appended_ref,
    weights,
    w_out,
    cache,
    stream,
    squares,
    part_a,
    part_b,
    sib_a,
    sib_b,
    z_a,
    z_b,
    turned,
    q_a,
    q_b,
    scores,
    seg_top,
    tops,
    ceilings,
    seg_num,
    seg_den,
    num,
    den,
    sib_num,
    sib_den,
    low_num,
    z_num,
    z_den,
    att_all,
    out_part,
    own_part,
    kv_part,
    out_rows,
    load_sem,
    sq_send,
    sq_recv,
    sib_send,
    sib_recv,
    z_send,
    z_recv,
    q_send,
    q_recv,
    top_send,
    top_recv,
    nsib_send,
    nsib_recv,
    nz_send,
    nz_recv,
    a_send,
    a_recv,
    kv_send,
    kv_recv,
    o_send,
    o_recv,
):
    n, kvn, steps, here, heads, hd, slots, width = sizes
    me = lax.axis_index("blk")
    kv = lax.axis_index("kv")
    chips = n // 2
    chip, core = me // 2, lax.rem(me, 2)
    sibling = me + 1 - 2 * core
    rows = steps * here
    beams = n * here
    quarter = n * rows // kvn
    half = heads // 2
    lanes = half * rows
    q_all = (q_a, q_b)
    parts, sib_parts, z_parts = (part_a, part_b), (sib_a, sib_b), (z_a, z_b)
    scaling = 1.0 / math.sqrt(hd)
    wide = w_out.shape[1]

    barrier = pltpu.get_barrier_semaphore()
    for d in range(1, n):
        pl.semaphore_signal(
            barrier, inc=1, device_id={"blk": lax.rem(me + d, n)}, device_id_type=MESH
        )
    for d in range(1, kvn):
        pl.semaphore_signal(
            barrier, inc=1, device_id={"kv": lax.rem(kv + d, kvn)}, device_id_type=MESH
        )
    hw = half * hd
    loads = [
        pltpu.make_async_copy(
            wq_hbm.at[:, pl.ds(0, hw)], weights.at[:, pl.ds(0, hw)], load_sem.at[0]
        ),
        pltpu.make_async_copy(wk_hbm, weights.at[:, pl.ds(hw, hd)], load_sem.at[1]),
        pltpu.make_async_copy(wv_hbm, weights.at[:, pl.ds(hw + hd, hd)], load_sem.at[2]),
        pltpu.make_async_copy(
            wq_hbm.at[:, pl.ds(hw, hw)], weights.at[:, pl.ds(hw + 2 * hd, hw)], load_sem.at[3]
        ),
        pltpu.make_async_copy(cache_hbm, cache, load_sem.at[4]),
        pltpu.make_async_copy(wo_hbm, w_out, load_sem.at[5]),
    ]
    for load in loads:
        load.start()

    x = embeds_ref[...].astype(jnp.float32)
    eye = lax.broadcasted_iota(jnp.int32, (beams, beams), 0) == lax.broadcasted_iota(
        jnp.int32, (beams, beams), 1
    )
    for s in range(steps):
        column = jnp.sum(x[s] * x[s], axis=1, keepdims=True)
        squares[0, s : s + 1, 0:beams] = jnp.sum(jnp.where(eye, column, 0.0), axis=0, keepdims=True)
    pl.semaphore_wait(barrier, n - 1 + kvn - 1)
    sends = []
    for d in range(1, n):
        sends.append(
            remote(
                squares.at[0], squares.at[d], sq_send.at[d], sq_recv.at[d], "blk", lax.rem(me + d, n)
            )
        )
        sends[-1].start()
    by_part = x.reshape(steps, n, here, wide).transpose(1, 0, 2, 3).reshape(n * rows, wide)
    stream[...] = by_part
    for send in sends:
        send.wait()
    normed = []
    for s in range(steps):
        total = squares[0, s : s + 1, 0:beams]
        for d in range(1, n):
            total = total + squares[d, s : s + 1, 0:beams]
        column = jnp.sum(jnp.where(eye, total, 0.0), axis=1, keepdims=True)
        normed.append(x[s] * lax.rsqrt(column / width + EPSILON) * gain_ref[...])
    normed = (
        jnp.stack(normed)
        .reshape(steps, chips, 2, here, wide)
        .transpose(2, 1, 0, 3, 4)
        .reshape(n * rows, wide)
        .astype(jnp.bfloat16)
    )
    for load in loads[:4]:
        load.wait()

    def across(source, target, send_sem, recv_sem):
        copies = []
        for d in range(1, chips):
            t = lax.rem(chip + d, chips)
            copies.append(
                remote(
                    source.at[t], target.at[d], send_sem.at[d], recv_sem.at[d], "blk", 2 * t + core
                )
            )
            copies[-1].start()
        return copies

    over = []
    first_column = 0
    for k in range(2):
        span = parts[k].shape[-1]
        parts[k][...] = jnp.dot(
            normed, weights[:, first_column : first_column + span], preferred_element_type=jnp.float32
        ).reshape(parts[k].shape)
        first_column += span
        over.append(
            remote(
                parts[k].at[1 - core], sib_parts[k], sib_send.at[k], sib_recv.at[k], "blk", sibling
            )
        )
        over[k].start()
    crossing = []
    for k in range(2):
        over[k].wait()
        sib_parts[k][...] = parts[k][core] + sib_parts[k][...]
        crossing.append(across(sib_parts[k], z_parts[k], z_send.at[k], z_recv.at[k]))
    loads[4].wait()

    def turn_values(i, carry):
        turned[i] = cache[i, 1].astype(jnp.float32).T.astype(jnp.bfloat16)
        return carry

    lax.fori_loop(0, slots, turn_values, 0, unroll=2)
    cos, sin = cos_ref[...], sin_ref[...]

    def rope(block):
        return block * cos + pltpu.roll(block, hd // 2, 1) * sin

    def arrived(k):
        for copy in crossing[k]:
            copy.wait()
        total = sib_parts[k][chip]
        for d in range(1, chips):
            total = total + z_parts[k][d]
        return total

    def spread(ref, send_sem, recv_sem):
        direct = []
        for d in range(1, chips):
            peer = 2 * lax.rem(chip + d, chips) + core
            direct.append(
                remote(ref.at[me], ref.at[me], send_sem.at[d], recv_sem.at[d], "blk", peer)
            )
            direct[-1].start()
        to_sibling = remote(
            ref.at[me], ref.at[me], send_sem.at[0], recv_sem.at[0], "blk", sibling
        )
        to_sibling.start()
        return direct, [to_sibling]

    def relay(ref, send_sem, recv_sem, copies):
        for d in range(1, chips):
            copies[0][d - 1].wait_recv()
            origin = 2 * lax.rem(chip + chips - d, chips) + core
            copies[1].append(
                remote(
                    ref.at[origin],
                    ref.at[origin],
                    send_sem.at[chips + d],
                    recv_sem.at[chips + d],
                    "blk",
                    sibling,
                )
            )
            copies[1][-1].start()

    def finish(copies):
        for copy in copies[1]:
            copy.wait()
        for copy in copies[0]:
            copy.wait_send()

    def turn_query(total):
        return jnp.concatenate(
            [rope(total[:, h * hd : (h + 1) * hd]) for h in range(half)], axis=0
        ).astype(jnp.bfloat16)

    queries, gathers = [None, None], [None, None]
    total = arrived(0)
    queries[0] = turn_query(total)
    q_all[0][me] = queries[0]
    gathers[0] = spread(q_all[0], q_send.at[0], q_recv.at[0])
    key = rope(total[:, half * hd : (half + 1) * hd]).astype(jnp.bfloat16)
    value_wide = total[:, (half + 1) * hd :]
    value = value_wide.astype(jnp.bfloat16)
    value_turned = value_wide.T.astype(jnp.bfloat16)
    entry = lax.broadcasted_iota(jnp.int32, (rows, lanes), 0)
    linked = jnp.zeros((rows, lanes), jnp.float32)
    for u in range(steps):
        seat = info_ref[me, 1 + u : 2 + u, :] + u * here
        known = info_ref[me, 1 + u : 2 + u, :] >= 0
        linked = jnp.where((entry == seat) & known, 1.0, linked)
    final = jnp.concatenate([linked[:, rows - here : rows]] * steps, axis=1)
    source = lax.broadcasted_iota(jnp.int32, (rows, rows), 0) // here
    wanted = lax.broadcasted_iota(jnp.int32, (rows, rows), 1) // here
    chosen = jnp.where(source == wanted, final, 0.0).T.astype(jnp.bfloat16)
    appended_ref[...] = jnp.dot(
        chosen, jnp.concatenate([key, value], axis=1), preferred_element_type=jnp.float32
    ).astype(jnp.bfloat16)
    queries[1] = turn_query(arrived(1))
    q_all[1][me] = queries[1]
    gathers[1] = spread(q_all[1], q_send.at[1], q_recv.at[1])
    relay(q_all[0], q_send.at[0], q_recv.at[0], gathers[0])

    contract_last = (((1,), (1,)), ((), ()))
    block = cache.shape[2]
    token = lax.broadcasted_iota(jnp.int32, (block, lanes), 0)
    own_scores, top_sends = [], []
    for k in range(2):
        own_scores.append(
            jnp.where(
                linked > 0,
                lax.dot_general(
                    key, queries[k], contract_last, preferred_element_type=jnp.float32
                )
                * scaling,
                NEGATIVE,
            )
        )
        own_top = jnp.max(own_scores[k], axis=0, keepdims=True)
        finish(gathers[k])

        def look(i, top):
            group = slot_ref[1 * slots + i]
            score = (
                lax.dot_general(
                    cache[slot_ref[i], 0],
                    q_all[k][group],
                    contract_last,
                    preferred_element_type=jnp.float32,
                )
                * scaling
            )
            limit = jnp.where(info_ref[group, 0:1, :] == slot_ref[2 * slots + i], slot_ref[3 * slots + i], 0)
            score = jnp.where(token < limit, score, NEGATIVE)
            scores[k, i] = score
            kept = jnp.where(slot_ref[4 * slots + i] > 0, top, NEGATIVE)
            top = jnp.maximum(kept, jnp.max(score, axis=0, keepdims=True))
            seg_top[i] = top
            return top

        lax.fori_loop(0, slots, look, jnp.full((1, lanes), NEGATIVE, jnp.float32), unroll=4)
        for g in range(n):
            top = jnp.where(slot_ref[5 * slots + n + g] > 0, seg_top[slot_ref[5 * slots + g]], NEGATIVE)
            tops[k, 0, g : g + 1, :] = jnp.where(me == g, jnp.maximum(top, own_top), top)
        copies = []
        for d in range(1, n):
            copies.append(
                remote(
                    tops.at[k, 0],
                    tops.at[k, d],
                    top_send.at[k, d],
                    top_recv.at[k, d],
                    "blk",
                    lax.rem(me + d, n),
                )
            )
            copies[-1].start()
        top_sends.append(copies)
        if k == 0:
            relay(q_all[1], q_send.at[1], q_recv.at[1], gathers[1])

    pairs, own_nums, own_dens = [], [], []

    def attend(k):
        for copy in top_sends[k]:
            copy.wait()
        ceiling = tops[k, 0]
        for d in range(1, n):
            ceiling = jnp.maximum(ceiling, tops[k, d])
        ceilings[...] = ceiling[:, None, :]

        def add(i, carry):
            total, count = carry
            probs = jnp.exp(scores[k, i] - ceilings[slot_ref[1 * slots + i]])
            same = slot_ref[4 * slots + i] > 0
            count = jnp.where(same, count, 0.0) + jnp.sum(probs, axis=0, keepdims=True)
            total = jnp.where(same, total, 0.0) + jnp.dot(
                turned[slot_ref[i]],
                probs.astype(jnp.bfloat16),
                preferred_element_type=jnp.float32,
            )
            seg_num[i] = total
            seg_den[i] = count
            return total, count

        lax.fori_loop(
            0,
            slots,
            add,
            (jnp.zeros((hd, lanes), jnp.float32), jnp.zeros((1, lanes), jnp.float32)),
            unroll=4,
        )
        own_probs = jnp.exp(own_scores[k] - ceilings[me])
        own_nums.append(
            jnp.dot(
                value_turned, own_probs.astype(jnp.bfloat16), preferred_element_type=jnp.float32
            ).T
        )
        own_dens.append(jnp.sum(own_probs, axis=0, keepdims=True))
        for t in range(chips):
            for c in range(2):
                g = 2 * t + c
                some = slot_ref[5 * slots + n + g] > 0
                num[k, c, t] = jnp.where(some, seg_num[slot_ref[5 * slots + g]], 0.0).T
                den[k, c, t] = jnp.where(some, seg_den[slot_ref[5 * slots + g]], 0.0)
        pair = [
            remote(
                num.at[k, 1 - core],
                sib_num.at[k],
                nsib_send.at[k, 0],
                nsib_recv.at[k, 0],
                "blk",
                sibling,
            ),
            remote(
                den.at[k, 1 - core],
                sib_den.at[k],
                nsib_send.at[k, 1],
                nsib_recv.at[k, 1],
                "blk",
                sibling,
            ),
        ]
        for copy in pair:
            copy.start()
        pairs.append(pair)

    def send_sums(k):
        for copy in pairs[k]:
            copy.wait()
        sib_num[k] = sib_num[k] + num[k, core]
        sib_den[k] = sib_den[k] + den[k, core]
        low_num[k] = sib_num[k].astype(jnp.bfloat16)
        return across(low_num.at[k], z_num.at[k], nz_send.at[k, 0], nz_recv.at[k, 0]) + across(
            sib_den.at[k], z_den.at[k], nz_send.at[k, 1], nz_recv.at[k, 1]
        )

    turn = lax.broadcasted_iota(jnp.int32, (lanes, lanes), 0) == lax.broadcasted_iota(
        jnp.int32, (lanes, lanes), 1
    )

    def close(k, copies):
        for copy in copies:
            copy.wait()
        numerator = own_nums[k] + sib_num[k, chip]
        denominator = own_dens[k] + sib_den[k, chip]
        for d in range(1, chips):
            numerator = numerator + z_num[k, d].astype(jnp.float32)
            denominator = denominator + z_den[k, d]
        column = jnp.sum(jnp.where(turn, denominator, 0.0), axis=1, keepdims=True)
        att_all[k, me] = (numerator / column).astype(jnp.bfloat16)
        return spread(att_all.at[k], a_send.at[k], a_recv.at[k])

    attend(0)
    sums = [send_sums(0)]
    attend(1)
    gathers = [close(0, sums[0])]
    sums.append(send_sums(1))
    relay(att_all.at[0], a_send.at[0], a_recv.at[0], gathers[0])
    gathers.append(close(1, sums[1]))
    loads[5].wait()

    def project(k):
        finish(gathers[k])
        attended = att_all[k].astype(jnp.float32).reshape(n, half, rows, hd)
        attended = jnp.concatenate(
            [attended[:, h].reshape(n * rows, hd) for h in range(half)], axis=1
        ).astype(jnp.bfloat16)
        return jnp.dot(
            attended,
            w_out[k * half * hd : (k + 1) * half * hd, :],
            preferred_element_type=jnp.float32,
        )

    early = project(0)
    relay(att_all.at[1], a_send.at[1], a_recv.at[1], gathers[1])
    out_sum = (early + project(1)).reshape(out_part.shape)
    out_part[...] = out_sum.astype(jnp.bfloat16)
    own_part[...] = out_sum
    sends = []
    for d in range(1, kvn):
        t = lax.rem(kv + d, kvn)
        sends.append(
            remote(out_part.at[t], kv_part.at[d], kv_send.at[d], kv_recv.at[d], "kv", t)
        )
        sends[-1].start()
    total = own_part[kv]
    for send in sends:
        send.wait()
    for d in range(1, kvn):
        total = total + kv_part[d].astype(jnp.float32)
    start = pl.multiple_of(kv * quarter, 16)
    out_rows[kv] = (stream[pl.ds(start, quarter)] + total).astype(jnp.bfloat16)
    sends = []
    for d in range(1, kvn):
        t = lax.rem(kv + d, kvn)
        sends.append(
            remote(out_rows.at[kv], out_rows.at[kv], o_send.at[d], o_recv.at[d], "kv", t)
        )
        sends[-1].start()
    for send in sends:
        send.wait()
    result = out_rows[...].astype(jnp.float32).reshape(n, steps, here, wide)
    out_ref[...] = result.transpose(1, 0, 2, 3).reshape(steps, beams, wide).astype(jnp.bfloat16)


def pick(table, index):
    count = table.shape[0]
    hit = index[:, None] == jnp.arange(count, dtype=jnp.int32)[None, :]
    return jnp.sum(jnp.where(hit, table[None, :], 0), axis=1)


def body(
    embeds, attn_gain, w_query, w_key, w_value, w_out, cache_kv, lengths, block_table, parents
):
    n = lax.axis_size("blk")
    kvn = lax.axis_size("kv")
    shard = lax.axis_index("blk")
    steps, beams, wide = embeds.shape
    here = beams // n
    slots = cache_kv.shape[0]
    block, hd = cache_kv.shape[3], cache_kv.shape[4]
    heads = w_query.shape[1] // hd
    rows = here * steps
    half = heads // 2
    lanes = half * rows
    all_beams = jnp.arange(beams, dtype=jnp.int32)
    roots, origin = [], []
    for s in range(steps):
        before = roots[-1] if s else all_beams
        roots.append(pick(before, parents[s]))
        origin.append([pick(line, parents[s]) for line in (origin[-1] if s else [])] + [all_beams])
    root = jnp.stack(roots)
    slot_ids = shard * slots + jnp.arange(slots, dtype=jnp.int32)
    named = block_table[None] == slot_ids[:, None, None]
    code = jnp.arange(block_table.size, dtype=jnp.int32).reshape(block_table.shape) + 1
    code = jnp.sum(jnp.where(named, code[None], 0), axis=(1, 2)) - 1
    filled = code >= 0
    owner = jnp.where(filled, code // block_table.shape[1], -1)
    logical = code % block_table.shape[1]
    tokens = jnp.where(filled, pick(lengths, jnp.maximum(owner, 0)) - logical * block, 0)
    group = jnp.where(filled, owner // GROUP, n - 1)
    place = jnp.arange(slots, dtype=jnp.int32)
    before = (group[None, :] == group[:, None]) & (place[None, :] < place[:, None])
    rank = jnp.sum((group[None, :] < group[:, None]) | before, axis=1)
    same = jnp.sum(before, axis=1)
    table = jnp.stack([place, group, owner, tokens, same.astype(jnp.int32)])
    table = jnp.sum(jnp.where((rank[:, None] == place[None, :])[None], table[:, :, None], 0), axis=1)
    every = jnp.arange(n, dtype=jnp.int32)[:, None]
    upto = jnp.sum(group[None, :] <= every, axis=1)
    held = jnp.sum(group[None, :] == every, axis=1)
    table = jnp.concatenate(
        [table.reshape(-1), jnp.maximum(upto - 1, 0), held], dtype=jnp.int32
    )
    base = all_beams // here * here
    info = jnp.stack(
        [
            jnp.stack([roots[s] if u < 0 else origin[s][u] - base if u <= s else base * 0 - 1
                       for s in range(steps)])
            for u in range(-1, steps)
        ]
    )
    info = info.reshape(1 + steps, steps, n, here).transpose(2, 0, 1, 3).reshape(n, 1 + steps, 1, rows)
    info = jnp.broadcast_to(info, (n, 1 + steps, half, rows)).reshape(n, 1 + steps, lanes)
    own = lax.dynamic_slice_in_dim(root, shard * here, here, 1)
    position = pick(lengths, own.reshape(-1)).reshape(steps, here) + jnp.arange(
        steps, dtype=jnp.int32
    )[:, None]
    lane = jnp.arange(hd, dtype=jnp.int32)
    exponent = (lane % (hd // 2)).astype(jnp.float32) * (2.0 / hd)
    angles = position.reshape(rows).astype(jnp.float32)[:, None] * (ROPE_BASE ** (-exponent))
    cos = jnp.cos(angles)
    sin = jnp.sin(angles) * jnp.where(lane < hd // 2, -1.0, 1.0)

    chips = n // 2
    total_rows = n * rows
    columns = (heads + 2) * hd
    quarter = total_rows // kvn
    sizes = (n, kvn, steps, here, heads, hd, slots, wide * n)
    bf16, f32 = jnp.bfloat16, jnp.float32
    dma = pltpu.SemaphoreType.DMA
    lane_room = -(-beams // 128) * 128
    vmem = pl.BlockSpec(memory_space=pltpu.VMEM)
    smem = pl.BlockSpec(memory_space=pltpu.SMEM)
    hbm = pl.BlockSpec(memory_space=pl.ANY)
    out, appended = pl.pallas_call(
        functools.partial(kernel, sizes),
        out_shape=(
            jax.ShapeDtypeStruct((steps, beams, wide), bf16),
            jax.ShapeDtypeStruct((rows, 2 * hd), bf16),
        ),
        in_specs=[smem] + [vmem] * 5 + [hbm] * 5,
        out_specs=(vmem, vmem),
        scratch_shapes=[
            pltpu.VMEM((wide, columns), bf16),
            pltpu.VMEM((heads * hd, wide), bf16),
            pltpu.VMEM((slots, 2, block, hd), bf16),
            pltpu.VMEM((total_rows, wide), f32),
            pltpu.VMEM((n, 8, lane_room), f32),
            pltpu.VMEM((2, chips, rows, (half + 2) * hd), f32),
            pltpu.VMEM((2, chips, rows, half * hd), f32),
            pltpu.VMEM((chips, rows, (half + 2) * hd), f32),
            pltpu.VMEM((chips, rows, half * hd), f32),
            pltpu.VMEM((chips, rows, (half + 2) * hd), f32),
            pltpu.VMEM((chips, rows, half * hd), f32),
            pltpu.VMEM((slots, hd, block), bf16),
            pltpu.VMEM((n, lanes, hd), bf16),
            pltpu.VMEM((n, lanes, hd), bf16),
            pltpu.VMEM((2, slots, block, lanes), f32),
            pltpu.VMEM((slots, 1, lanes), f32),
            pltpu.VMEM((2, n, n, lanes), f32),
            pltpu.VMEM((n, 1, lanes), f32),
            pltpu.VMEM((slots, hd, lanes), f32),
            pltpu.VMEM((slots, 1, lanes), f32),
            pltpu.VMEM((2, 2, chips, lanes, hd), f32),
            pltpu.VMEM((2, 2, chips, 1, lanes), f32),
            pltpu.VMEM((2, chips, lanes, hd), f32),
            pltpu.VMEM((2, chips, 1, lanes), f32),
            pltpu.VMEM((2, chips, lanes, hd), bf16),
            pltpu.VMEM((2, chips, lanes, hd), bf16),
            pltpu.VMEM((2, chips, 1, lanes), f32),
            pltpu.VMEM((2, n, lanes, hd), bf16),
            pltpu.VMEM((kvn, quarter, wide), bf16),
            pltpu.VMEM((kvn, quarter, wide), f32),
            pltpu.VMEM((kvn, quarter, wide), bf16),
            pltpu.VMEM((kvn, quarter, wide), bf16),
            dma((6,)),
            dma((n,)),
            dma((n,)),
            dma((2,)),
            dma((2,)),
            dma((2, chips)),
            dma((2, chips)),
            dma((2, n)),
            dma((2, n)),
            dma((2, n)),
            dma((2, n)),
            dma((2, 2)),
            dma((2, 2)),
            dma((2, 2, chips)),
            dma((2, 2, chips)),
            dma((2, n)),
            dma((2, n)),
            dma((kvn,)),
            dma((kvn,)),
            dma((kvn,)),
            dma((kvn,)),
        ],
        compiler_params=pltpu.CompilerParams(
            collective_id=0, has_side_effects=True, vmem_limit_bytes=60 * 1024 * 1024
        ),
    )(
        table,
        embeds,
        attn_gain[None, :],
        info,
        cos,
        sin,
        w_query,
        w_key,
        w_value,
        w_out,
        cache_kv.reshape(slots, 2, block, hd),
    )
    return out, appended.reshape(steps, here, 1, 2, hd)


def solution(mesh):
    return jax.shard_map(
        body,
        mesh=mesh,
        in_specs=(
            P(None, None, "blk"),
            P("blk"),
            P("blk", "kv"),
            P("blk", "kv"),
            P("blk", "kv"),
            P("kv", "blk"),
            P("blk", "kv", None, None, None),
            P(),
            P(),
            P(),
        ),
        out_specs=(P(None, None, "blk"), P(None, "blk", "kv", None, None)),
        check_vma=False,
    )
```
